256 devices in a mesh: seq: 64 (over z, x, core), head: 4 (over y).
Axes of the slice: x: 4, y: 4, z: 8, core: 2. Of those that a mesh axis runs over, the one named last changes fastest.
Arguments:
- query_key: bfloat16 [32768, 128], P('seq'), may hold values from -1.5 to 1.5
- values: bfloat16 [32768, 5120], P('seq', 'head'), may hold values from -0.119628906 to 0.119628906
- cotangent: bfloat16 [32768, 5120], P('seq', 'head'), may hold values from -0.119628906 to 0.119628906
- level_gain: float32 [16, 15, 80], P(None, None, 'head'), may hold values from 0.1 to 1
- level_code: int32 [512], P('seq'), may hold values from 0 to 15
Outputs:
- mixed: bfloat16 [32768, 5120], P('seq', 'head')
- grad_qk: float32 [32768, 128], P('seq')
- grad_values: bfloat16 [32768, 5120], P('seq', 'head')
The draws below stay inside these ranges and needn't reach their ends.
Inputs may be any that keep to these rules, and one draw needn't show every extreme that they name: `level_code`: each span's row of the weight table.
All inputs are finite; a program needn't handle non-finite values.
Results may differ from the reference program's by a relative error of at most 0.005.
Values sent between devices are 32-bit elements; how exact they have to be, the bound alone decides.
No kernel may reach another device: no remote copies, remote signals or barrier semaphores. Data moves between devices by JAX's collectives and lax.ppermute only.
A program may use at most 128 MiB of HBM per device.

```python
import math
import jax
import jax.numpy as jnp
from jax import lax

HEADS = 80
HEAD_DIM = 64
STATE = 128
CH = 64
LEVELS = 15
CODES = 16
TOK_DEV = 512
TOKENS = 32768
SPANS = 512
SEQ_LEVELS = 6
SPAN_LEVELS = 3
N_SEQ = 64
N_HEAD = 4


def place_ends(values, rng, smallest, largest):
    spot = [jax.random.randint(jax.random.fold_in(rng, axis), (), 0, length) for axis, length in enumerate(values.shape)]
    widest = values.shape.index(max(values.shape))
    next_to = spot[:widest] + [(spot[widest] + 1) % values.shape[widest]] + spot[widest + 1:]
    return values.at[tuple(spot)].set(smallest).at[tuple(next_to)].set(largest)


def shard_levels(stream_key, dims, pieces, smallest, largest):
    def one(position, shards_of):
        draws = jax.random.uniform(jax.random.fold_in(jax.random.fold_in(stream_key, 6), position), (shards_of,), jnp.float32, smallest / len(pieces), largest / len(pieces))
        return jnp.repeat(jnp.exp(draws), dims[position] // shards_of).reshape((-1,) + (1,) * (len(dims) - position - 1))

    loudness = one(*pieces[0])
    for cut in pieces[1:]:
        loudness = loudness * one(*cut)
    return loudness


def normal_values(stream_key, extent, scale, reach, cuts=(), kind=jnp.bfloat16):
    entries = scale * jax.random.normal(stream_key, extent, jnp.float32)
    if cuts:
        entries = entries * shard_levels(stream_key, extent, cuts, -0.22, 0.18)
    return jnp.clip(entries, -reach, reach).astype(kind)


def setup_inputs(seed: int = 0) -> dict:
    streams_of = jax.random.split(jax.random.key(seed), 6)
    return {
        "query_key": normal_values(streams_of[0], (TOKENS, STATE), 0.25, 1.5, ((0, 64),)),
        "values": normal_values(streams_of[1], (TOKENS, HEADS * HEAD_DIM), 0.02, 0.119628906, ((0, 64), (1, 4))),
        "cotangent": normal_values(streams_of[2], (TOKENS, HEADS * HEAD_DIM), 0.02, 0.119628906, ((0, 64), (1, 4))),
        "level_gain": jnp.clip(jnp.exp(math.log(1.0) - 2.3025851 * jax.random.uniform(streams_of[3], (CODES, LEVELS, HEADS), jnp.float32) ** shard_levels(streams_of[3], (CODES, LEVELS, HEADS), ((2, 4),), -0.2, 0.2)), 0.1, 1.0),
        "level_code": place_ends(jax.random.randint(streams_of[4], (SPANS,), 0, CODES), jax.random.fold_in(streams_of[4], 1), 0, CODES - 1).astype(jnp.int32),
    }


precise = lax.Precision.HIGHEST


def bit_length(numbers, top_bits):
    bit_total = jnp.zeros_like(numbers)
    for bit_power in range(top_bits):
        bit_total = bit_total + (numbers >= (1 << bit_power)).astype(jnp.int32)
    return bit_total


def local_levels(span_count):
    span_ids = jnp.arange(span_count, dtype=jnp.int32)
    return bit_length(span_ids[:, None] ^ span_ids[None, :], 8)


def segment_pass(q_seg, val_seg, cot_seg, weight_seg, sibling, adjoint):
    groups = weight_seg.shape[-1]
    span_count = TOK_DEV // CH
    cross_weight = weight_seg[:, SPAN_LEVELS + 1:SPAN_LEVELS + 1 + SEQ_LEVELS, :]
    cross_cols = jnp.repeat(cross_weight, HEAD_DIM, axis=-1)
    summed = jnp.einsum('clj,lij->cij', cross_cols, sibling, precision=precise)
    span_state = lax.optimization_barrier(summed.astype(jnp.bfloat16)).astype(jnp.float32)
    onehot = (local_levels(span_count)[:, :, None] == jnp.arange(SPAN_LEVELS + 1, dtype=jnp.int32)[None, None, :]).astype(jnp.float32)
    local_weight = jnp.einsum('abk,akg->gab', onehot, weight_seg[:, :SPAN_LEVELS + 1, :], precision=precise)
    weight = jnp.broadcast_to(local_weight[:, :, None, :, None], (groups, span_count, CH, span_count, CH)).reshape(groups, TOK_DEV, TOK_DEV)
    causal = jnp.tril(jnp.ones((TOK_DEV, TOK_DEV), dtype=bool))
    q_float = q_seg.astype(jnp.float32)
    scores = jnp.dot(q_seg, q_seg.T, preferred_element_type=jnp.float32)
    mixing = lax.optimization_barrier(jnp.where(causal, weight * scores, 0.0).astype(jnp.bfloat16)).astype(jnp.float32)
    v_float = val_seg.astype(jnp.float32).reshape(TOK_DEV, groups, HEAD_DIM)
    c_float = cot_seg.astype(jnp.float32).reshape(TOK_DEV, groups, HEAD_DIM)
    inner_out = jnp.einsum('gts,sgp->tgp', mixing, v_float).reshape(TOK_DEV, groups * HEAD_DIM)
    q_spans = q_float.reshape(span_count, CH, STATE)
    outer_out = jnp.einsum('cti,cij->ctj', q_spans, span_state).reshape(TOK_DEV, groups * HEAD_DIM)
    mixed_seg = (inner_out + outer_out).astype(jnp.bfloat16)
    d_mix = jnp.einsum('tgp,sgp->gts', c_float, v_float)
    d_score = jnp.sum(jnp.where(causal, weight * d_mix, 0.0), axis=0)
    dq_inner = jnp.dot(d_score, q_float, precision=precise) + jnp.dot(d_score.T, q_float, precision=precise)
    dv_inner = jnp.einsum('gts,tgp->sgp', mixing, c_float).reshape(TOK_DEV, groups * HEAD_DIM)
    c_spans = c_float.reshape(span_count, CH, groups * HEAD_DIM)
    dq_outer = jnp.einsum('ctj,cij->cti', c_spans, span_state).reshape(TOK_DEV, STATE)
    adjoint_bf = lax.optimization_barrier(adjoint.astype(jnp.bfloat16)).astype(jnp.float32)
    dv_outer = jnp.dot(q_float, adjoint_bf)
    dk_outer = jnp.dot(v_float.reshape(TOK_DEV, groups * HEAD_DIM), adjoint_bf.T)
    grad_q_seg = dq_inner + dq_outer + dk_outer
    grad_v_seg = (dv_inner + dv_outer).astype(jnp.bfloat16)
    return mixed_seg, grad_v_seg, grad_q_seg


def group_pass(query_key, val_group, cot_group, weight_group):
    span_count = TOK_DEV // CH
    groups = weight_group.shape[-1]
    cols = groups * HEAD_DIM
    q_segs = query_key.reshape(N_SEQ, TOK_DEV, STATE)
    v_segs = val_group.reshape(N_SEQ, TOK_DEV, cols)
    c_segs = cot_group.reshape(N_SEQ, TOK_DEV, cols)
    q_f = q_segs.astype(jnp.float32)
    own_state = jnp.einsum('eti,etj->eij', q_f, v_segs.astype(jnp.float32))
    span_grad = jnp.einsum('ecti,ectj->ecij', q_f.reshape(N_SEQ, span_count, CH, STATE), c_segs.astype(jnp.float32).reshape(N_SEQ, span_count, CH, cols))
    weight_segs = weight_group.reshape(N_SEQ, span_count, LEVELS, groups)
    cross_cols = jnp.repeat(weight_segs[:, :, SPAN_LEVELS + 1:SPAN_LEVELS + 1 + SEQ_LEVELS, :], HEAD_DIM, axis=-1)
    level_grad = jnp.einsum('ecij,eclj->leij', span_grad, cross_cols, precision=precise)
    siblings = []
    adjoint = jnp.zeros((N_SEQ, STATE, cols), dtype=jnp.float32)
    for level in range(1, SEQ_LEVELS + 1):
        half_len = 1 << (level - 1)
        blocks = N_SEQ >> level
        halves_view = own_state.reshape(blocks, 2, half_len, STATE, cols)
        low_sum = jnp.sum(halves_view[:, 0], axis=1, keepdims=True)
        filled = jnp.broadcast_to(low_sum[:, :, None], (blocks, 1, half_len, STATE, cols))
        siblings.append(jnp.concatenate([jnp.zeros_like(filled), filled], axis=1).reshape(N_SEQ, STATE, cols))
        grad_view = level_grad[level - 1].reshape(blocks, 2, half_len, STATE, cols)
        high_sum = jnp.sum(grad_view[:, 1], axis=1, keepdims=True)
        spread = jnp.broadcast_to(high_sum[:, :, None], (blocks, 1, half_len, STATE, cols))
        adjoint = adjoint + jnp.concatenate([spread, jnp.zeros_like(spread)], axis=1).reshape(N_SEQ, STATE, cols)
    sibling = jnp.stack(siblings, axis=1)

    def one_segment(items):
        return segment_pass(*items)

    mixed_g, grad_v_g, grad_q_g = lax.map(one_segment, (q_segs, v_segs, c_segs, weight_segs, sibling, adjoint))
    return mixed_g.reshape(TOKENS, cols), grad_v_g.reshape(TOKENS, cols), grad_q_g.reshape(TOKENS, STATE)


def reference(query_key, values, cotangent, level_gain, level_code):
    groups = HEADS // N_HEAD
    cols = groups * HEAD_DIM
    span_weight = level_gain[level_code]
    span_weight = span_weight.reshape(SPANS, LEVELS, N_HEAD, groups).transpose(2, 0, 1, 3)
    val_groups = values.reshape(TOKENS, N_HEAD, cols).transpose(1, 0, 2)
    cot_groups = cotangent.reshape(TOKENS, N_HEAD, cols).transpose(1, 0, 2)

    def one_group(items):
        return group_pass(query_key, items[0], items[1], items[2])

    mixed_all, grad_v_all, grad_q_all = lax.map(one_group, (val_groups, cot_groups, span_weight))
    mixed = mixed_all.transpose(1, 0, 2).reshape(TOKENS, HEADS * HEAD_DIM)
    grad_values = grad_v_all.transpose(1, 0, 2).reshape(TOKENS, HEADS * HEAD_DIM)
    grad_qk = jnp.sum(grad_q_all, axis=0)
    return mixed, grad_qk, grad_values
```

```python
import jax
import jax.numpy as jnp
from jax import lax
from jax.experimental import pallas as pl
from jax.experimental.pallas import tpu as pltpu
from jax.sharding import PartitionSpec as P

HEAD_DIM = 64
CH = 64
TOK = 512
STATE = 128
COLS = 1280
HEADS = COLS // HEAD_DIM
BLK = 256
STEPS = COLS // BLK
SPANS = TOK // CH
USED = 10
TILE = 256
BF = jnp.bfloat16
F32 = jnp.float32
ROW, CORE, XMASK, ZLOW = 8, 1, 3, 1

LOCAL = ((0, 0, 0), (0, 0, 1), (0, 0, 2), (1, 1, 0), (1, 1, 1), (1, 1, 2), (1, 0, 3))


def send(value, mask, axis="seq"):
    pairs = [(source, source ^ mask) for source in range(lax.axis_size(axis))]
    return lax.ppermute(value, axis, pairs)


def dot(a, b, over_a, over_b):
    return lax.dot_general(a, b, (((over_a,), (over_b,)), ((), ())), preferred_element_type=F32)


def coords():
    position = lax.axis_index("seq")
    return position, position & CORE, (position >> 1) & XMASK, (position >> 3) & ZLOW


def params():
    return pltpu.CompilerParams(
        dimension_semantics=("arbitrary",), vmem_limit_bytes=48 * 1024 * 1024
    )


def cols(*lead):
    rank = len(lead)
    return pl.BlockSpec(lead + (BLK,), lambda j: (0,) * rank + (j,))


def whole(*shape):
    return pl.BlockSpec(shape, lambda j: (0,) * len(shape))


def cost(macs, moved):
    return pl.CostEstimate(flops=2 * macs, bytes_accessed=moved, transcendentals=0)


def write_scaled(z_ref, index, w_ref, level, e_ref):
    for a in range(SPANS):
        rows = slice(a * CH, (a + 1) * CH)
        z_ref[index, rows, :] = (w_ref[level, a : a + 1, :] * e_ref[rows, :].astype(F32)).astype(BF)


def level_operand(z_ref, index, k, position, w_ref, v_ref, e_ref):
    upper = (position >> (k - 1)) & 1

    @pl.when(upper == 1)
    def _():
        write_scaled(z_ref, index, w_ref, k + 3, e_ref)

    @pl.when(upper == 0)
    def _():
        z_ref[index] = v_ref[...]


def far_kernel(code_ref, gain_ref, q_ref, v_ref, e_ref, w_ref, z_ref, own_ref, oth_ref, qt, lw, res):
    position, core, x, z0 = coords()
    step = pl.program_id(0)

    @pl.when(step == 0)
    def _():
        qt[...] = q_ref[...].T
        lw[...] = jnp.zeros_like(lw)
        for a in range(SPANS):
            lw[0:15, a, 0:HEADS] = gain_ref[code_ref[a]]

    weights = lw[...].reshape(16 * SPANS, 128)
    head = lax.broadcasted_iota(jnp.int32, (128, BLK), 0)
    col = lax.broadcasted_iota(jnp.int32, (128, BLK), 1) + step * BLK
    spread = (head == col // HEAD_DIM).astype(BF)
    high = weights.astype(BF)
    rest = weights - high.astype(F32)
    middle = rest.astype(BF)
    low = (rest - middle.astype(F32)).astype(BF)
    wide = dot(high, spread, 1, 0) + (dot(middle, spread, 1, 0) + dot(low, spread, 1, 0))
    w_ref[...] = wide.reshape(16, SPANS, BLK)[:USED]
    for index, k in enumerate((4, 5, 6)):
        level_operand(z_ref, index, k, position, w_ref, v_ref, e_ref)
        res[...] = dot(qt[...], z_ref[index], 1, 0).reshape(16, ROW, BLK)
        for xr in range(4):
            for zr in range(2):
                slot = 4 + zr if k == 4 else 2 * zr + (k - 5)
                place = ((xr ^ x) << 1) | (zr if k == 4 else zr ^ z0)
                own_ref[xr, slot] = res[(core << 3) | place]
                oth_ref[xr, slot] = res[((core ^ 1) << 3) | place]


def far_states(code, gain, q, v, e):
    return pl.pallas_call(
        far_kernel,
        grid=(STEPS,),
        in_specs=[
            pl.BlockSpec(memory_space=pltpu.SMEM),
            whole(16, 15, HEADS),
            whole(TOK, STATE),
            cols(TOK),
            cols(TOK),
        ],
        out_specs=[cols(USED, SPANS), cols(3, TOK), cols(4, 6, ROW), cols(4, 6, ROW)],
        out_shape=[
            jax.ShapeDtypeStruct((USED, SPANS, COLS), F32),
            jax.ShapeDtypeStruct((3, TOK, COLS), BF),
            jax.ShapeDtypeStruct((4, 6, ROW, COLS), F32),
            jax.ShapeDtypeStruct((4, 6, ROW, COLS), F32),
        ],
        scratch_shapes=[
            pltpu.VMEM((STATE, TOK), BF),
            pltpu.VMEM((16, SPANS, 128), F32),
            pltpu.VMEM((16, ROW, BLK), F32),
        ],
        compiler_params=params(),
        cost_estimate=cost(3 * TOK * STATE * COLS, 9 << 20),
        name="far_states",
    )(code, gain, q, v, e)


def near_kernel(q_ref, v_ref, e_ref, w_ref, z_ref, x_ref, own_ref, oth_ref, qt, res):
    position, core, x, z0 = coords()

    @pl.when(pl.program_id(0) == 0)
    def _():
        qt[...] = q_ref[...].T

    for index, k in enumerate((2, 3, 1)):
        level_operand(z_ref, index, k, position, w_ref, v_ref, e_ref)
        if k == 1:
            x_ref[...] = dot(qt[...], z_ref[index], 1, 0)
        else:
            res[...] = dot(qt[...], z_ref[index], 1, 0).reshape(2, STATE // 2, BLK)
            own_ref[k - 2] = res[core]
            oth_ref[k - 2] = res[core ^ 1]


def near_states(q, v, e, w):
    half = STATE // 2
    return pl.pallas_call(
        near_kernel,
        grid=(STEPS,),
        in_specs=[whole(TOK, STATE), cols(TOK), cols(TOK), cols(USED, SPANS)],
        out_specs=[cols(3, TOK), cols(STATE), cols(2, half), cols(2, half)],
        out_shape=[
            jax.ShapeDtypeStruct((3, TOK, COLS), BF),
            jax.ShapeDtypeStruct((STATE, COLS), F32),
            jax.ShapeDtypeStruct((2, half, COLS), F32),
            jax.ShapeDtypeStruct((2, half, COLS), F32),
        ],
        scratch_shapes=[pltpu.VMEM((STATE, TOK), BF), pltpu.VMEM((2, half, BLK), F32)],
        compiler_params=params(),
        cost_estimate=cost(3 * TOK * STATE * COLS, 9 << 20),
        name="near_states",
    )(q, v, e, w)


def kept(level, flip):
    rows = lax.broadcasted_iota(jnp.int32, (TILE, TILE), 1 if flip else 0)
    keys = lax.broadcasted_iota(jnp.int32, (TILE, TILE), 0 if flip else 1)
    a, b = rows // CH, keys // CH
    if level == 0:
        return (a == b) & (keys <= rows)
    return ((a ^ b) >> (level - 1) == 1) & (a > b)


def local_kernel(q_ref, v_ref, e_ref, w_ref, m_ref, d_ref, dq_ref, score, flipped, grad, z):
    step = pl.program_id(0)

    @pl.when(step == 0)
    def _():
        grad[...] = jnp.zeros_like(grad)
        for index, (t, s, level) in enumerate(LOCAL):
            qt_rows = q_ref[t * TILE : (t + 1) * TILE, :]
            qs_rows = q_ref[s * TILE : (s + 1) * TILE, :]
            direct = dot(qt_rows, qs_rows, 1, 1)
            swapped = dot(qs_rows, qt_rows, 1, 1)
            if level < 3:
                direct = jnp.where(kept(level, False), direct, 0.0)
                swapped = jnp.where(kept(level, True), swapped, 0.0)
            score[index] = direct.astype(BF)
            flipped[index] = swapped.astype(BF)

    mixed = [None, None]
    d_val = [None, None]
    per = TILE // CH
    for index, (t, s, level) in enumerate(LOCAL):
        vals = v_ref[s * TILE : (s + 1) * TILE, :]
        for a in range(per):
            rows = slice(t * TILE + a * CH, t * TILE + (a + 1) * CH)
            w_row = w_ref[level, t * per + a : t * per + a + 1, :]
            z[index, a * CH : (a + 1) * CH, :] = (w_row * e_ref[rows, :].astype(F32)).astype(BF)
        out = dot(score[index], vals, 1, 0)
        w_rows = jnp.concatenate(
            [
                jnp.broadcast_to(w_ref[level, t * per + a : t * per + a + 1, :], (CH, BLK))
                for a in range(per)
            ],
            axis=0,
        )
        out = w_rows * out
        back = dot(flipped[index], z[index], 1, 0)
        mixed[t] = out if mixed[t] is None else mixed[t] + out
        d_val[s] = back if d_val[s] is None else d_val[s] + back
        grad[index] += dot(z[index], vals, 1, 1)
    for i in range(2):
        m_ref[i * TILE : (i + 1) * TILE, :] = mixed[i]
        d_ref[i * TILE : (i + 1) * TILE, :] = d_val[i]

    @pl.when(step == STEPS - 1)
    def _():
        q = [q_ref[i * TILE : (i + 1) * TILE, :] for i in range(2)]
        cross = grad[6].astype(BF)
        extra = [dot(cross, q[1], 0, 0), dot(cross, q[0], 1, 0)]
        for i in range(2):
            total = jnp.zeros((TILE, TILE), F32)
            for level in range(3):
                total = total + jnp.where(kept(level, False), grad[3 * i + level], 0.0)
            total = total.astype(BF)
            part = dot(total, q[i], 1, 0) + dot(total, q[i], 0, 0)
            dq_ref[i * TILE : (i + 1) * TILE, :] = part + extra[i]


def local_part(q, v, e, w):
    return pl.pallas_call(
        local_kernel,
        grid=(STEPS,),
        in_specs=[whole(TOK, STATE), cols(TOK), cols(TOK), cols(USED, SPANS)],
        out_specs=[cols(TOK), cols(TOK), whole(TOK, STATE)],
        out_shape=[
            jax.ShapeDtypeStruct((TOK, COLS), F32),
            jax.ShapeDtypeStruct((TOK, COLS), F32),
            jax.ShapeDtypeStruct((TOK, STATE), F32),
        ],
        scratch_shapes=[
            pltpu.VMEM((7, TILE, TILE), BF),
            pltpu.VMEM((7, TILE, TILE), BF),
            pltpu.VMEM((7, TILE, TILE), F32),
            pltpu.VMEM((7, TILE, BLK), BF),
        ],
        compiler_params=params(),
        cost_estimate=cost(21 * TILE * TILE * COLS, 9 << 20),
        name="local_part",
    )(q, v, e, w)


def add_outer(q_ref, w_ref, k, position, state, m_ref, d_ref, first, m_in, d_in):
    upper = (position >> (k - 1)) & 1
    out = dot(q_ref[...], state, 1, 0)
    to_value = (1 - upper).astype(F32)
    to_mixed = upper.astype(F32)
    for a in range(SPANS):
        rows = slice(a * CH, (a + 1) * CH)
        w_row = w_ref[k + 3, a : a + 1, :] * to_mixed
        m_old = m_in[rows, :] if first else m_ref[rows, :]
        d_old = d_in[rows, :] if first else d_ref[rows, :]
        m_ref[rows, :] = m_old + w_row * out[rows, :]
        d_ref[rows, :] = d_old + to_value * out[rows, :]


def mid_kernel(*refs):
    (q_ref, w_ref, m_in, d_in, dq_in, zn_ref, zf_ref, y1_ref, y23_ref, y23o_ref, y4_ref, y4o_ref) = refs[:12]
    m_ref, d_ref, dq_ref, y = refs[12:]
    position, core, x, z0 = coords()
    step = pl.program_id(0)

    @pl.when(step == 0)
    def _():
        dq_ref[...] = dq_in[...]

    for index, k in enumerate((2, 3)):
        y[index, core] = y23_ref[index]
        y[index, core ^ 1] = y23o_ref[index]
    for xr in range(4):
        part = (x ^ xr) * 16
        rows = pl.ds(pl.multiple_of(part, 16), 16)
        y[2, core, rows, :] = y4_ref[xr].reshape(16, BLK)
        y[2, core ^ 1, rows, :] = y4o_ref[xr].reshape(16, BLK)
    grads = None
    for index, k in enumerate((2, 3, 4, 1)):
        state = (y1_ref[...] if k == 1 else y[index].reshape(STATE, BLK)).astype(BF)
        z = zf_ref[0] if k == 4 else zn_ref[2 if k == 1 else index]
        add_outer(q_ref, w_ref, k, position, state, m_ref, d_ref, index == 0, m_in, d_in)
        part = dot(z, state, 1, 1)
        grads = part if grads is None else grads + part
    dq_ref[...] += grads


def mid_part(q, w, m, d, dq, zn, zf, y1, y23, y23o, y4, y4o):
    half = STATE // 2
    return pl.pallas_call(
        mid_kernel,
        grid=(STEPS,),
        in_specs=[
            whole(TOK, STATE),
            cols(USED, SPANS),
            cols(TOK),
            cols(TOK),
            whole(TOK, STATE),
            cols(3, TOK),
            cols(1, TOK),
            cols(STATE),
            cols(2, half),
            cols(2, half),
            cols(4, 2, ROW),
            cols(4, 2, ROW),
        ],
        out_specs=[cols(TOK), cols(TOK), whole(TOK, STATE)],
        out_shape=[
            jax.ShapeDtypeStruct((TOK, COLS), F32),
            jax.ShapeDtypeStruct((TOK, COLS), F32),
            jax.ShapeDtypeStruct((TOK, STATE), F32),
        ],
        scratch_shapes=[pltpu.VMEM((3, 2, half, BLK), F32)],
        compiler_params=params(),
        cost_estimate=cost(8 * TOK * STATE * COLS, 18 << 20),
        name="mid_part",
    )(q, w, m, d, dq, zn, zf, y1, y23, y23o, y4, y4o)


def gather_far(y, refs):
    position, core, x, z0 = coords()
    for cr in range(2):
        for xr in range(4):
            for zr in range(2):
                place = ((cr ^ core) << 3) | ((xr ^ x) << 1) | (zr ^ z0)
                for index in range(2):
                    y[index, place] = refs[4 * cr + xr][2 * zr + index]


def score_kernel(*refs):
    dq_in, z_ref = refs[:2]
    dq_ref, y = refs[10:]

    @pl.when(pl.program_id(0) == 0)
    def _():
        dq_ref[...] = dq_in[...]

    gather_far(y, refs[2:10])
    grads = None
    for index in range(2):
        state = y[index].reshape(STATE, BLK).astype(BF)
        part = dot(z_ref[1 + index], state, 1, 1)
        grads = part if grads is None else grads + part
    dq_ref[...] += grads


def score_part(dq, zf, pieces):
    return pl.pallas_call(
        score_kernel,
        grid=(STEPS,),
        in_specs=[whole(TOK, STATE), cols(3, TOK)] + [cols(4, ROW)] * 8,
        out_specs=whole(TOK, STATE),
        out_shape=jax.ShapeDtypeStruct((TOK, STATE), F32),
        scratch_shapes=[pltpu.VMEM((2, 16, ROW, BLK), F32)],
        compiler_params=params(),
        cost_estimate=cost(2 * TOK * STATE * COLS, 5 << 20),
        name="score_part",
    )(dq, zf, *pieces)


def last_kernel(*refs):
    q_ref, w_ref, m_in, d_in = refs[:4]
    mixed_ref, dv_ref, m_ref, d_ref, y = refs[12:]
    position, core, x, z0 = coords()
    gather_far(y, refs[4:12])
    for index, k in enumerate((5, 6)):
        state = y[index].reshape(STATE, BLK).astype(BF)
        add_outer(q_ref, w_ref, k, position, state, m_ref, d_ref, index == 0, m_in, d_in)
    mixed_ref[...] = m_ref[...].astype(BF)
    dv_ref[...] = d_ref[...].astype(BF)


def last_part(q, w, m, d, pieces):
    return pl.pallas_call(
        last_kernel,
        grid=(STEPS,),
        in_specs=[whole(TOK, STATE), cols(USED, SPANS), cols(TOK), cols(TOK)] + [cols(4, ROW)] * 8,
        out_specs=[cols(TOK), cols(TOK)],
        out_shape=[
            jax.ShapeDtypeStruct((TOK, COLS), BF),
            jax.ShapeDtypeStruct((TOK, COLS), BF),
        ],
        scratch_shapes=[
            pltpu.VMEM((TOK, BLK), F32),
            pltpu.VMEM((TOK, BLK), F32),
            pltpu.VMEM((2, 16, ROW, BLK), F32),
        ],
        compiler_params=params(),
        cost_estimate=cost(2 * TOK * STATE * COLS, 10 << 20),
        name="last_part",
    )(q, w, m, d, *pieces)


def local(q, v, e, gain, code):
    w, zf, own_f, oth_f = far_states(code, gain, q, v, e)
    got_f = send(oth_f, 1)
    zn, x1, own_n, oth_n = near_states(q, v, e, w)
    got_n = send(oth_n, 1)
    y1 = send(x1, 1)

    chip = [own_f[j] + got_f[j] for j in range(4)]
    slices = [send(chip[j], 2 * j) for j in (1, 2, 3)]
    m, d, dq = local_part(q, v, e, w)
    near = [own_n[i] + got_n[i] for i in range(2)]
    piece = chip[0] + slices[0] + slices[1] + slices[2]
    piece, near = lax.optimization_barrier((piece, near))

    low = send(piece[2:6], 8)
    y2 = send(near[0], 2)
    y3 = send(near[1], 4) + send(near[1], 6)
    y4 = low[2:4]
    five = piece[0] + low[0]
    six = piece[1] + low[1]
    y5 = send(five, 16)
    y6 = send(six, 32) + send(six, 48)
    y4s = jnp.stack([y4] + [send(y4, 2 * j) for j in (1, 2, 3)])
    y4o = send(y4s, 1)
    y23 = jnp.stack([y2, y3])
    y23o = send(y23, 1)

    half = jnp.stack([y5, y6])
    quad = jnp.concatenate([half, send(half, 8)])
    pieces = [quad] + [send(quad, 2 * j) for j in (1, 2, 3)]
    pieces = pieces + [send(p, 1) for p in pieces]
    m, d, dq = mid_part(q, w, m, d, dq, zn, zf, y1, y23, y23o, y4s, y4o)
    dq = score_part(dq, zf, pieces)
    parts = [dq] + [send(dq, h, "head") for h in (1, 2, 3)]
    mixed, grad_values = last_part(q, w, m, d, pieces)
    grad_qk = (parts[0] + parts[1]) + (parts[2] + parts[3])
    return mixed, grad_qk, grad_values


def solution(mesh):
    placed = (P("seq", None), P("seq", "head"), P("seq", "head"), P(None, None, "head"), P("seq"))
    return jax.shard_map(
        local,
        mesh=mesh,
        in_specs=placed,
        out_specs=(P("seq", "head"), P("seq", None), P("seq", "head")),
        check_vma=False,
    )
```

```python
import functools

import jax
import jax.numpy as jnp
from jax import lax
from jax.experimental import pallas as pl
from jax.experimental.pallas import tpu as pltpu
from jax.sharding import PartitionSpec as P

HEAD_DIM = 64
CH = 64
TOK = 512
STATE = 128
COLS = 1280
HEADS = COLS // HEAD_DIM
BLK = 256
STEPS = COLS // BLK
SPANS = TOK // CH
USED = 10
TILE = 256
BF = jnp.bfloat16
F32 = jnp.float32
ROW, CORE, XMASK = 8, 1, 3
BLOCKS = tuple(slice(j * BLK, (j + 1) * BLK) for j in range(STEPS))

LOCAL = ((0, 0, 0), (0, 0, 1), (0, 0, 2), (1, 1, 0), (1, 1, 1), (1, 1, 2), (1, 0, 3))


def send(value, mask, axis="seq"):
    pairs = [(source, source ^ mask) for source in range(lax.axis_size(axis))]
    return lax.ppermute(value, axis, pairs)


def dot(a, b, over_a, over_b):
    return lax.dot_general(a, b, (((over_a,), (over_b,)), ((), ())), preferred_element_type=F32)


def coords():
    position = lax.axis_index("seq")
    return position, position & CORE, (position >> 1) & XMASK, (position >> 3) & CORE


def params(mib):
    return pltpu.CompilerParams(vmem_limit_bytes=mib * 1024 * 1024)


def cost(macs, moved):
    return pl.CostEstimate(flops=2 * macs, bytes_accessed=moved, transcendentals=0)


def shape(*dims, kind=F32):
    return jax.ShapeDtypeStruct(dims, kind)


VMEM = pl.BlockSpec(memory_space=pltpu.VMEM)
SMEM = pl.BlockSpec(memory_space=pltpu.SMEM)
HBM = pl.BlockSpec(memory_space=pltpu.HBM)


def level_operand(z_ref, index, k, position, w_ref, v_ref, e_ref, block):
    upper = (position >> (k - 1)) & 1

    @pl.when(upper == 1)
    def _():
        for a in range(SPANS):
            rows = slice(a * CH, (a + 1) * CH)
            scaled = w_ref[k + 3, a : a + 1, block] * e_ref[rows, block].astype(F32)
            z_ref[index, rows, block] = scaled.astype(BF)

    @pl.when(upper == 0)
    def _():
        z_ref[index, :, block] = v_ref[:, block]


def far_kernel(
    code_hbm, gain_hbm, q_hbm, v_hbm, e_hbm, w_ref, q_ref, v_ref, e_ref, z_ref, own_ref, oth_ref,
    code_ref, gain_ref, qt, lw, res, sems
):
    position, core, x, z0 = coords()
    first = []
    for i, (far, near) in enumerate(((code_hbm, code_ref), (gain_hbm, gain_ref), (q_hbm, q_ref))):
        copy = pltpu.make_async_copy(far, near, sems.at[2 * STEPS + i])
        copy.start()
        first.append(copy)
    copies = []
    for j, block in enumerate(BLOCKS):
        for i, (far, near) in enumerate(((v_hbm, v_ref), (e_hbm, e_ref))):
            copy = pltpu.make_async_copy(far.at[:, block], near.at[:, block], sems.at[2 * j + i])
            copy.start()
            copies.append(copy)
    lw[...] = jnp.zeros_like(lw)
    for copy in first:
        copy.wait()
    for a in range(SPANS):
        lw[0:15, a, 0:HEADS] = gain_ref[code_ref[a]]
    weights = lw[...].reshape(16 * SPANS, 128)[: USED * SPANS]
    high = weights.astype(BF)
    rest = weights - high.astype(F32)
    middle = rest.astype(BF)
    low = (rest - middle.astype(F32)).astype(BF)
    head = lax.broadcasted_iota(jnp.int32, (128, BLK), 0)
    for j, block in enumerate(BLOCKS):
        col = lax.broadcasted_iota(jnp.int32, (128, BLK), 1) + j * BLK
        spread = (head == col // HEAD_DIM).astype(BF)
        wide = dot(high, spread, 1, 0) + (dot(middle, spread, 1, 0) + dot(low, spread, 1, 0))
        w_ref[:, :, block] = wide.reshape(USED, SPANS, BLK)
    qt[...] = q_ref[...].T
    for j, block in enumerate(BLOCKS):
        copies[2 * j].wait()
        copies[2 * j + 1].wait()
        for index, k in enumerate((5, 6, 4)):
            level_operand(z_ref, index, k, position, w_ref, v_ref, e_ref, block)
            res[...] = dot(qt[...], z_ref[index, :, block], 1, 0).reshape(8, 2, ROW, BLK)
            for xr in range(4):
                for zr in range(2):
                    slot = 4 + zr if k == 4 else 2 * zr + index
                    half = zr if k == 4 else zr ^ z0
                    own_ref[xr, slot, :, block] = res[(core << 2) | (xr ^ x), half]
                    oth_ref[xr, slot, :, block] = res[((core ^ 1) << 2) | (xr ^ x), half]


def far_states(code, gain, q, v, e):
    return pl.pallas_call(
        far_kernel,
        in_specs=[HBM] * 5,
        out_specs=[VMEM] * 7,
        out_shape=[
            shape(USED, SPANS, COLS),
            shape(TOK, STATE, kind=BF),
            shape(TOK, COLS, kind=BF),
            shape(TOK, COLS, kind=BF),
            shape(3, TOK, COLS, kind=BF),
            shape(4, 6, ROW, COLS),
            shape(4, 6, ROW, COLS),
        ],
        scratch_shapes=[
            pltpu.SMEM((SPANS,), jnp.int32),
            pltpu.VMEM((16, 15, HEADS), F32),
            pltpu.VMEM((STATE, TOK), BF),
            pltpu.VMEM((16, SPANS, 128), F32),
            pltpu.VMEM((8, 2, ROW, BLK), F32),
            pltpu.SemaphoreType.DMA((2 * STEPS + 3,)),
        ],
        compiler_params=params(20),
        cost_estimate=cost(3 * TOK * STATE * COLS, 9 << 20),
        name="far_states",
    )(code, gain, q, v, e)


def near_kernel(q_ref, v_ref, e_ref, w_ref, z_ref, x_ref, own_ref, oth_ref, qt, res):
    position, core, x, z0 = coords()
    qt[...] = q_ref[...].T
    for index, k in enumerate((2, 3, 1)):
        for block in BLOCKS:
            level_operand(z_ref, index, k, position, w_ref, v_ref, e_ref, block)
            out = dot(qt[...], z_ref[index, :, block], 1, 0)
            if k == 1:
                x_ref[:, block] = out
            else:
                res[...] = out.reshape(2, STATE // 2, BLK)
                own_ref[k - 2, :, block] = res[core]
                oth_ref[k - 2, :, block] = res[core ^ 1]


def near_states(q, v, e, w):
    half = STATE // 2
    return pl.pallas_call(
        near_kernel,
        in_specs=[VMEM] * 4,
        out_specs=[VMEM] * 4,
        out_shape=[
            shape(3, TOK, COLS, kind=BF),
            shape(STATE, COLS),
            shape(2, half, COLS),
            shape(2, half, COLS),
        ],
        scratch_shapes=[pltpu.VMEM((STATE, TOK), BF), pltpu.VMEM((2, half, BLK), F32)],
        compiler_params=params(20),
        cost_estimate=cost(3 * TOK * STATE * COLS, 9 << 20),
        name="near_states",
    )(q, v, e, w)


def kept(level, flip):
    rows = lax.broadcasted_iota(jnp.int32, (TILE, TILE), 1 if flip else 0)
    keys = lax.broadcasted_iota(jnp.int32, (TILE, TILE), 0 if flip else 1)
    a, b = rows // CH, keys // CH
    if level == 0:
        return (a == b) & (keys <= rows)
    return ((a ^ b) >> (level - 1) == 1) & (a > b)


def add_outer(q_ref, w_ref, k, position, state, m_ref, d_ref, block):
    upper = (position >> (k - 1)) & 1

    @pl.when(upper == 1)
    def _():
        out = dot(q_ref[...], state, 1, 0)
        for a in range(SPANS):
            rows = slice(a * CH, (a + 1) * CH)
            m_ref[rows, block] += w_ref[k + 3, a : a + 1, block] * out[rows, :]

    @pl.when(upper == 0)
    def _():
        d_ref[:, block] += dot(q_ref[...], state, 1, 0)


def local_kernel(q_ref, v_ref, e_ref, w_ref, zn_ref, y1_ref, m_ref, d_ref, dq_ref, score, flipped, grad, z):
    position, core, x, z0 = coords()
    dq_ref[...] = jnp.zeros_like(dq_ref)
    grad[...] = jnp.zeros_like(grad)
    for index, (t, s, level) in enumerate(LOCAL):
        qt_rows = q_ref[t * TILE : (t + 1) * TILE, :]
        qs_rows = q_ref[s * TILE : (s + 1) * TILE, :]
        direct = dot(qt_rows, qs_rows, 1, 1)
        swapped = dot(qs_rows, qt_rows, 1, 1)
        if level < 3:
            direct = jnp.where(kept(level, False), direct, 0.0)
            swapped = jnp.where(kept(level, True), swapped, 0.0)
        score[index] = direct.astype(BF)
        flipped[index] = swapped.astype(BF)

    per = TILE // CH

    def one_block(j, carry):
        block = pl.ds(pl.multiple_of(j * BLK, BLK), BLK)
        mixed = [None, None]
        d_val = [None, None]
        for index, (t, s, level) in enumerate(LOCAL):
            vals = v_ref[s * TILE : (s + 1) * TILE, block]
            for a in range(per):
                rows = slice(t * TILE + a * CH, t * TILE + (a + 1) * CH)
                w_row = w_ref[level, t * per + a : t * per + a + 1, block]
                z[index, a * CH : (a + 1) * CH, :] = (w_row * e_ref[rows, block].astype(F32)).astype(BF)
            out = dot(score[index], vals, 1, 0)
            w_rows = jnp.concatenate(
                [
                    jnp.broadcast_to(w_ref[level, t * per + a : t * per + a + 1, block], (CH, BLK))
                    for a in range(per)
                ],
                axis=0,
            )
            out = w_rows * out
            back = dot(flipped[index], z[index], 1, 0)
            mixed[t] = out if mixed[t] is None else mixed[t] + out
            d_val[s] = back if d_val[s] is None else d_val[s] + back
            grad[index] += dot(z[index], vals, 1, 1)
        for i in range(2):
            m_ref[i * TILE : (i + 1) * TILE, block] = mixed[i]
            d_ref[i * TILE : (i + 1) * TILE, block] = d_val[i]
        state = y1_ref[:, block].astype(BF)
        add_outer(q_ref, w_ref, 1, position, state, m_ref, d_ref, block)
        dq_ref[...] += dot(zn_ref[2, :, block], state, 1, 1)
        return carry

    lax.fori_loop(0, STEPS, one_block, 0)
    q = [q_ref[i * TILE : (i + 1) * TILE, :] for i in range(2)]
    cross = grad[6].astype(BF)
    extra = [dot(cross, q[1], 0, 0), dot(cross, q[0], 1, 0)]
    for i in range(2):
        total = jnp.zeros((TILE, TILE), F32)
        for level in range(3):
            total = total + jnp.where(kept(level, False), grad[3 * i + level], 0.0)
        total = total.astype(BF)
        part = dot(total, q[i], 1, 0) + dot(total, q[i], 0, 0)
        dq_ref[i * TILE : (i + 1) * TILE, :] += part + extra[i]


def local_part(q, v, e, w, zn, y1):
    return pl.pallas_call(
        local_kernel,
        in_specs=[VMEM] * 6,
        out_specs=[VMEM] * 3,
        out_shape=[shape(TOK, COLS), shape(TOK, COLS), shape(TOK, STATE)],
        scratch_shapes=[
            pltpu.VMEM((7, TILE, TILE), BF),
            pltpu.VMEM((7, TILE, TILE), BF),
            pltpu.VMEM((7, TILE, TILE), F32),
            pltpu.VMEM((7, TILE, BLK), BF),
        ],
        compiler_params=params(20),
        cost_estimate=cost(25 * TILE * TILE * COLS, 9 << 20),
        name="local_part",
    )(q, v, e, w, zn, y1)


def mid_kernel(q_ref, w_ref, m_in, d_in, dq_in, z_ref, y2_ref, y3_ref, y23o_ref, m_ref, d_ref, dq_ref, y):
    position, core, x, z0 = coords()
    for index, ref in enumerate((y2_ref, y3_ref)):
        y[index, core] = ref[...].astype(BF)
        y[index, core ^ 1] = y23o_ref[index].astype(BF)
    grads = dq_in[...]
    for block in BLOCKS:
        m_ref[:, block] = m_in[:, block]
        d_ref[:, block] = d_in[:, block]
        for index, k in enumerate((2, 3)):
            state = y[index, :, :, block].reshape(STATE, BLK)
            add_outer(q_ref, w_ref, k, position, state, m_ref, d_ref, block)
            grads = grads + dot(z_ref[index, :, block], state, 1, 1)
    dq_ref[...] = grads


def mid_part(q, w, m, d, dq, z, y2, y3, y23o):
    return pl.pallas_call(
        mid_kernel,
        in_specs=[VMEM] * 9,
        out_specs=[VMEM] * 3,
        out_shape=[shape(TOK, COLS), shape(TOK, COLS), shape(TOK, STATE)],
        input_output_aliases={2: 0, 3: 1},
        scratch_shapes=[pltpu.VMEM((2, 2, STATE // 2, COLS), BF)],
        compiler_params=params(30),
        cost_estimate=cost(4 * TOK * STATE * COLS, 18 << 20),
        name="mid_part",
    )(q, w, m, d, dq, z, y2, y3, y23o)


def score_kernel(*refs):
    dq_in, z_ref = refs[:2]
    pieces = refs[2:10]
    parts, y, total = refs[10:14], refs[14], refs[15]
    position, core, x, z0 = coords()
    group = lax.axis_index("head")
    for cr in range(2):
        for xr in range(4):
            piece = pieces[4 * cr + xr]
            place = ((cr ^ core) << 2) | (xr ^ x)
            rows = pl.ds(pl.multiple_of(place * 16, 16), 16)
            for index in range(2):
                pair = [piece[2 * z0 + index], piece[2 * (1 - z0) + index]]
                y[index, rows, :] = jnp.concatenate(pair, axis=0).astype(BF)
            y[2, rows, :] = piece[4:6].reshape(16, COLS).astype(BF)
    grads = dq_in[...]
    for index in range(3):
        for block in BLOCKS:
            grads = grads + dot(z_ref[index, :, block], y[index, :, block], 1, 1)
    total[...] = grads.reshape(4, TOK // 4, STATE)
    for j in range(4):
        parts[j][...] = total[group ^ j]


def score_part(dq, z, pieces):
    part = shape(TOK // 4, STATE)
    return pl.pallas_call(
        score_kernel,
        in_specs=[VMEM] * 10,
        out_specs=[VMEM] * 5,
        out_shape=[part, part, part, part, shape(3, STATE, COLS, kind=BF)],
        scratch_shapes=[pltpu.VMEM((4, TOK // 4, STATE), F32)],
        compiler_params=params(20),
        cost_estimate=cost(3 * TOK * STATE * COLS, 5 << 20),
        name="score_part",
    )(dq, z, *pieces)


def join_kernel(a_ref, b_ref, c_ref, d_ref, out_ref):
    group = lax.axis_index("head")
    for j, ref in enumerate((a_ref, b_ref, c_ref, d_ref)):
        rows = pl.ds(pl.multiple_of((group ^ j) * (TOK // 4), TOK // 4), TOK // 4)
        out_ref[rows, :] = ref[...]


def join(parts):
    return pl.pallas_call(
        join_kernel,
        in_specs=[VMEM] * 4,
        out_specs=VMEM,
        out_shape=shape(TOK, STATE),
        compiler_params=params(8),
        cost_estimate=cost(0, 1 << 19),
        name="join",
    )(*parts)


def last_kernel(keep, q_ref, w_ref, in_ref, y_ref, out_ref, acc):
    position, core, x, z0 = coords()
    for block in BLOCKS:
        acc[:, block] = in_ref[:, block]
        for index, k in enumerate((5, 6, 4)):

            @pl.when((position >> (k - 1)) & 1 == keep)
            def _():
                out = dot(q_ref[...], y_ref[index, :, block], 1, 0)
                if keep == 0:
                    acc[:, block] += out
                else:
                    for a in range(SPANS):
                        rows = slice(a * CH, (a + 1) * CH)
                        acc[rows, block] += w_ref[k + 3, a : a + 1, block] * out[rows, :]

        out_ref[:, block] = acc[:, block].astype(BF)


def last_part(keep, q, w, before, y):
    return pl.pallas_call(
        functools.partial(last_kernel, keep),
        in_specs=[VMEM] * 4,
        out_specs=VMEM,
        out_shape=shape(TOK, COLS, kind=BF),
        scratch_shapes=[pltpu.VMEM((TOK, COLS), F32)],
        compiler_params=params(20),
        cost_estimate=cost(3 * TOK * STATE * COLS // 2, 5 << 20),
        name="last_mixed" if keep else "last_values",
    )(q, w, before, y)


def local(q_hbm, v_hbm, e_hbm, gain, code):
    tie = lax.optimization_barrier
    w, q, v, e, zf, own_f, oth_f = far_states(code, gain, q_hbm, v_hbm, e_hbm)
    got_f = send(oth_f, 1)
    zn, x1, own_n, oth_n = near_states(q, v, e, w)

    chip = [own_f[j] + got_f[j] for j in range(4)]
    chip, oth_n, x1 = tie((chip, oth_n, x1))
    slices = [send(chip[j], 2 * j) for j in (1, 2, 3)]
    got_n = send(oth_n, 1)
    y1 = send(x1, 1)
    m, d, dq = local_part(q, v, e, w, zn, y1)
    near = [own_n[i] + got_n[i] for i in range(2)]
    slices, near, m, d, dq = tie((slices, near, m, d, dq))
    mine = [sum((s[i] for s in slices), chip[0][i]) for i in range(2)]
    other = sum((s[2:6] for s in slices), chip[0][2:6])

    low = send(other, 8)
    y2 = send(near[0], 2)
    y3 = [send(near[1], 4), send(near[1], 6)]
    five = mine[0] + low[0]
    six = mine[1] + low[1]
    y5 = send(five, 16)
    y6 = send(six, 32) + send(six, 48)
    half = jnp.stack([y5, y6])
    rest = send(half, 8)
    rest, y2, y3 = tie((rest, y2, y3))
    quad = jnp.concatenate([half, rest, low[2:4]])
    y3 = y3[0] + y3[1]
    quad, y2, y3, dq = tie((quad, y2, y3, dq))
    pieces = [quad] + [send(quad, 2 * j) for j in (1, 2, 3)]
    y23o = send(jnp.stack([y2, y3]), 1)
    m, d, dq = mid_part(q, w, m, d, dq, zn, y2, y3, y23o)
    pieces, dq = tie((pieces, dq))
    pieces = pieces + [send(p, 1) for p in pieces]
    *parts, y = score_part(dq, zf, pieces)
    got = [send(parts[h], h, "head") for h in (1, 2, 3)]
    grad_values = last_part(0, q, w, d, y)
    got, grad_values = tie((got, grad_values))
    total = (parts[0] + got[0]) + (got[1] + got[2])
    total, m = tie((total, m))
    parts = [total] + [send(total, h, "head") for h in (1, 2, 3)]
    mixed = last_part(1, q, w, m, y)
    parts, mixed = tie((parts, mixed))
    return mixed, join(parts), grad_values


def solution(mesh):
    placed = (P("seq", None), P("seq", "head"), P("seq", "head"), P(None, None, "head"), P("seq"))
    return jax.shard_map(
        local,
        mesh=mesh,
        in_specs=placed,
        out_specs=(P("seq", "head"), P("seq", None), P("seq", "head")),
        check_vma=False,
    )
```

```python
import functools

import jax
import jax.numpy as jnp
from jax import lax
from jax.experimental import pallas as pl
from jax.experimental.pallas import tpu as pltpu
from jax.sharding import PartitionSpec as P

HEAD_DIM = 64
CH = 64
TOK = 512
STATE = 128
COLS = 1280
HEADS = COLS // HEAD_DIM
BLK = 256
STEPS = COLS // BLK
SPANS = TOK // CH
USED = 10
TILE = 256
BF = jnp.bfloat16
F32 = jnp.float32
ROW, CORE, XMASK = 8, 1, 3
BLOCKS = tuple(slice(j * BLK, (j + 1) * BLK) for j in range(STEPS))

LOCAL = ((0, 0, 0), (0, 0, 1), (0, 0, 2), (1, 1, 0), (1, 1, 1), (1, 1, 2), (1, 0, 3))


def send(value, mask, axis="seq"):
    pairs = [(source, source ^ mask) for source in range(lax.axis_size(axis))]
    return lax.ppermute(value, axis, pairs)


def dot(a, b, over_a, over_b):
    return lax.dot_general(a, b, (((over_a,), (over_b,)), ((), ())), preferred_element_type=F32)


def coords():
    position = lax.axis_index("seq")
    return position, position & CORE, (position >> 1) & XMASK, (position >> 3) & CORE


def params(mib):
    return pltpu.CompilerParams(vmem_limit_bytes=mib * 1024 * 1024)


def cost():
    return pl.CostEstimate(flops=1024, bytes_accessed=1024, transcendentals=0)


def shape(*dims, kind=F32):
    return jax.ShapeDtypeStruct(dims, kind)


VMEM = pl.BlockSpec(memory_space=pltpu.VMEM)
SMEM = pl.BlockSpec(memory_space=pltpu.SMEM)
HBM = pl.BlockSpec(memory_space=pltpu.HBM)


def level_operand(z_ref, index, k, position, w_ref, v_ref, e_ref, block):
    upper = (position >> (k - 1)) & 1

    @pl.when(upper == 1)
    def _():
        for a in range(SPANS):
            rows = slice(a * CH, (a + 1) * CH)
            scaled = w_ref[k + 3, a : a + 1, block] * e_ref[rows, block].astype(F32)
            z_ref[index, rows, block] = scaled.astype(BF)

    @pl.when(upper == 0)
    def _():
        z_ref[index, :, block] = v_ref[:, block]


def near_kernel(
    code_hbm, gain_hbm, q_hbm, v_hbm, e_hbm, w_ref, q_ref, qt, v_ref, e_ref, z_ref, own_ref, oth_ref,
    code_ref, gain_ref, lw, res, sems
):
    position, core, x, z0 = coords()
    first = []
    for i, (far, near) in enumerate(((code_hbm, code_ref), (gain_hbm, gain_ref), (q_hbm, q_ref))):
        copy = pltpu.make_async_copy(far, near, sems.at[2 * STEPS + i])
        copy.start()
        first.append(copy)
    copies = []
    for j, block in enumerate(BLOCKS):
        for i, (far, near) in enumerate(((v_hbm, v_ref), (e_hbm, e_ref))):
            copy = pltpu.make_async_copy(far.at[:, block], near.at[:, block], sems.at[2 * j + i])
            copy.start()
            copies.append(copy)
    lw[...] = jnp.zeros_like(lw)
    for copy in first:
        copy.wait()
    for a in range(SPANS):
        lw[0:15, a : a + 1, 0:HEADS] = gain_ref[:, pl.ds(code_ref[a], 1), :]
    weights = lw[...].reshape(16 * SPANS, 128)[: USED * SPANS]
    high = weights.astype(BF)
    rest = weights - high.astype(F32)
    middle = rest.astype(BF)
    low = (rest - middle.astype(F32)).astype(BF)
    head = lax.broadcasted_iota(jnp.int32, (128, BLK), 0)
    for j, block in enumerate(BLOCKS):
        col = lax.broadcasted_iota(jnp.int32, (128, BLK), 1) + j * BLK
        spread = (head == col // HEAD_DIM).astype(BF)
        wide = dot(high, spread, 1, 0) + (dot(middle, spread, 1, 0) + dot(low, spread, 1, 0))
        w_ref[:, :, block] = wide.reshape(USED, SPANS, BLK)
    qt[...] = q_ref[...].T
    for j, block in enumerate(BLOCKS):
        copies[2 * j].wait()
        copies[2 * j + 1].wait()
        for index, k in enumerate((2, 3)):
            level_operand(z_ref, index, k, position, w_ref, v_ref, e_ref, block)
            res[...] = dot(qt[...], z_ref[index, :, block], 1, 0).reshape(2, STATE // 2, BLK)
            own_ref[index, :, block] = res[core]
            oth_ref[index, :, block] = res[core ^ 1]


def near_states(code, gain, q, v, e):
    half = STATE // 2
    return pl.pallas_call(
        near_kernel,
        in_specs=[HBM] * 5,
        out_specs=[VMEM] * 8,
        out_shape=[
            shape(USED, SPANS, COLS),
            shape(TOK, STATE, kind=BF),
            shape(STATE, TOK, kind=BF),
            shape(TOK, COLS, kind=BF),
            shape(TOK, COLS, kind=BF),
            shape(2, TOK, COLS, kind=BF),
            shape(2, half, COLS),
            shape(2, half, COLS),
        ],
        scratch_shapes=[
            pltpu.SMEM((SPANS,), jnp.int32),
            pltpu.VMEM((15, 16, HEADS), F32),
            pltpu.VMEM((16, SPANS, 128), F32),
            pltpu.VMEM((2, half, BLK), F32),
            pltpu.SemaphoreType.DMA((2 * STEPS + 3,)),
        ],
        compiler_params=params(20),
        cost_estimate=cost(),
        name="near_states",
    )(code, gain, q, v, e)


def far_kernel(qt, v_ref, e_ref, w_ref, z_ref, own_ref, oth_ref, res):
    position, core, x, z0 = coords()
    for block in BLOCKS:
        for index, k in enumerate((5, 6)):
            level_operand(z_ref, index, k, position, w_ref, v_ref, e_ref, block)
            res[...] = dot(qt[...], z_ref[index, :, block], 1, 0).reshape(8, 2, ROW, BLK)
            for xr in range(4):
                for zr in range(2):
                    own_ref[xr, 2 * zr + index, :, block] = res[(core << 2) | (xr ^ x), zr ^ z0]
                    oth_ref[xr, 2 * zr + index, :, block] = res[((core ^ 1) << 2) | (xr ^ x), zr ^ z0]
    own_ref[:, 4:6] = jnp.zeros((4, 2, ROW, COLS), F32)
    oth_ref[:, 4:6] = jnp.zeros((4, 2, ROW, COLS), F32)


def far_states(qt, v, e, w):
    return pl.pallas_call(
        far_kernel,
        in_specs=[VMEM] * 4,
        out_specs=[VMEM] * 3,
        out_shape=[
            shape(2, TOK, COLS, kind=BF),
            shape(4, 6, ROW, COLS),
            shape(4, 6, ROW, COLS),
        ],
        scratch_shapes=[pltpu.VMEM((8, 2, ROW, BLK), F32)],
        compiler_params=params(20),
        cost_estimate=cost(),
        name="far_states",
    )(qt, v, e, w)


def rest_kernel(qt, v_ref, e_ref, w_ref, own_in, oth_in, z_ref, own_ref, oth_ref, x_ref, res):
    position, core, x, z0 = coords()
    own_ref[:, 0:4] = own_in[:, 0:4]
    oth_ref[:, 0:4] = oth_in[:, 0:4]
    for block in BLOCKS:
        for index, k in enumerate((4, 1)):
            level_operand(z_ref, index, k, position, w_ref, v_ref, e_ref, block)
            out = dot(qt[...], z_ref[index, :, block], 1, 0)
            if k == 1:
                x_ref[:, block] = out
                continue
            res[...] = out.reshape(8, 2, ROW, BLK)
            for xr in range(4):
                own_ref[xr, 4:6, :, block] = res[(core << 2) | (xr ^ x)]
                oth_ref[xr, 4:6, :, block] = res[((core ^ 1) << 2) | (xr ^ x)]


def rest_states(qt, v, e, w, own, oth):
    return pl.pallas_call(
        rest_kernel,
        in_specs=[VMEM] * 6,
        out_specs=[VMEM] * 4,
        out_shape=[
            shape(2, TOK, COLS, kind=BF),
            shape(4, 6, ROW, COLS),
            shape(4, 6, ROW, COLS),
            shape(STATE, COLS),
        ],
        scratch_shapes=[pltpu.VMEM((8, 2, ROW, BLK), F32)],
        compiler_params=params(20),
        cost_estimate=cost(),
        name="rest_states",
    )(qt, v, e, w, own, oth)


def kept(level, flip):
    rows = lax.broadcasted_iota(jnp.int32, (TILE, TILE), 1 if flip else 0)
    keys = lax.broadcasted_iota(jnp.int32, (TILE, TILE), 0 if flip else 1)
    a, b = rows // CH, keys // CH
    if level == 0:
        return (a == b) & (keys <= rows)
    return ((a ^ b) >> (level - 1) == 1) & (a > b)


def add_outer(q_ref, w_ref, levels, position, y_ref, m_ref, d_ref, block):
    for index, k in enumerate(levels):

        @pl.when((position >> (k - 1)) & 1 == 1)
        def _():
            out = dot(q_ref[...], y_ref[index, :, block].astype(BF), 1, 0)
            for a in range(SPANS):
                rows = slice(a * CH, (a + 1) * CH)
                m_ref[rows, block] += w_ref[k + 3, a : a + 1, block] * out[rows, :]

    lower = None
    for index, k in enumerate(levels):
        part = (1 - ((position >> (k - 1)) & 1)).astype(F32) * y_ref[index, :, block]
        lower = part if lower is None else lower + part
    d_ref[:, block] += dot(q_ref[...], lower.astype(BF), 1, 0)


def local_kernel(q_ref, v_ref, e_ref, w_ref, zr_ref, y1_ref, m_ref, d_ref, dq_ref, score, flipped, grad, z, y):
    y[0] = y1_ref[...]
    position, core, x, z0 = coords()
    dq_ref[...] = jnp.zeros_like(dq_ref)
    grad[...] = jnp.zeros_like(grad)
    for index, (t, s, level) in enumerate(LOCAL):
        qt_rows = q_ref[t * TILE : (t + 1) * TILE, :]
        qs_rows = q_ref[s * TILE : (s + 1) * TILE, :]
        direct = dot(qt_rows, qs_rows, 1, 1)
        swapped = dot(qs_rows, qt_rows, 1, 1)
        if level < 3:
            direct = jnp.where(kept(level, False), direct, 0.0)
            swapped = jnp.where(kept(level, True), swapped, 0.0)
        score[index] = direct.astype(BF)
        flipped[index] = swapped.astype(BF)

    per = TILE // CH

    def one_block(j, carry):
        block = pl.ds(pl.multiple_of(j * BLK, BLK), BLK)
        mixed = [None, None]
        d_val = [None, None]
        for index, (t, s, level) in enumerate(LOCAL):
            vals = v_ref[s * TILE : (s + 1) * TILE, block]
            for a in range(per):
                rows = slice(t * TILE + a * CH, t * TILE + (a + 1) * CH)
                w_row = w_ref[level, t * per + a : t * per + a + 1, block]
                z[index, a * CH : (a + 1) * CH, :] = (w_row * e_ref[rows, block].astype(F32)).astype(BF)
            out = dot(score[index], vals, 1, 0)
            w_rows = jnp.concatenate(
                [
                    jnp.broadcast_to(w_ref[level, t * per + a : t * per + a + 1, block], (CH, BLK))
                    for a in range(per)
                ],
                axis=0,
            )
            out = w_rows * out
            back = dot(flipped[index], z[index], 1, 0)
            mixed[t] = out if mixed[t] is None else mixed[t] + out
            d_val[s] = back if d_val[s] is None else d_val[s] + back
            grad[index] += dot(z[index], vals, 1, 1)
        for i in range(2):
            m_ref[i * TILE : (i + 1) * TILE, block] = mixed[i]
            d_ref[i * TILE : (i + 1) * TILE, block] = d_val[i]
        add_outer(q_ref, w_ref, (1,), position, y, m_ref, d_ref, block)
        dq_ref[...] += dot(zr_ref[1, :, block], y[0, :, block].astype(BF), 1, 1)
        return carry

    lax.fori_loop(0, STEPS, one_block, 0)
    q = [q_ref[i * TILE : (i + 1) * TILE, :] for i in range(2)]
    cross = grad[6].astype(BF)
    extra = [dot(cross, q[1], 0, 0), dot(cross, q[0], 1, 0)]
    for i in range(2):
        total = jnp.zeros((TILE, TILE), F32)
        for level in range(3):
            total = total + jnp.where(kept(level, False), grad[3 * i + level], 0.0)
        total = total.astype(BF)
        part = dot(total, q[i], 1, 0) + dot(total, q[i], 0, 0)
        dq_ref[i * TILE : (i + 1) * TILE, :] += part + extra[i]


def local_part(q, v, e, w, zr, y1):
    return pl.pallas_call(
        local_kernel,
        in_specs=[VMEM] * 6,
        out_specs=[VMEM] * 3,
        out_shape=[shape(TOK, COLS), shape(TOK, COLS), shape(TOK, STATE)],
        scratch_shapes=[
            pltpu.VMEM((7, TILE, TILE), BF),
            pltpu.VMEM((7, TILE, TILE), BF),
            pltpu.VMEM((7, TILE, TILE), F32),
            pltpu.VMEM((7, TILE, BLK), BF),
            pltpu.VMEM((1, STATE, COLS), F32),
        ],
        compiler_params=params(20),
        cost_estimate=cost(),
        name="local_part",
    )(q, v, e, w, zr, y1)


def mid_kernel(q_ref, w_ref, m_in, d_in, dq_in, z_ref, y2_ref, y3_ref, y23o_ref, m_ref, d_ref, dq_ref, y):
    position, core, x, z0 = coords()
    half = STATE // 2
    own = pl.ds(pl.multiple_of(core * half, half), half)
    oth = pl.ds(pl.multiple_of((core ^ 1) * half, half), half)
    for index, ref in enumerate((y2_ref, y3_ref)):
        y[index, own, :] = ref[...]
        y[index, oth, :] = y23o_ref[index]
    grads = dq_in[...]
    for block in BLOCKS:
        m_ref[:, block] = m_in[:, block]
        d_ref[:, block] = d_in[:, block]
        add_outer(q_ref, w_ref, (2, 3), position, y, m_ref, d_ref, block)
        for index in range(2):
            grads = grads + dot(z_ref[index, :, block], y[index, :, block].astype(BF), 1, 1)
    dq_ref[...] = grads


def mid_part(q, w, m, d, dq, zn, y2, y3, y23o):
    return pl.pallas_call(
        mid_kernel,
        in_specs=[VMEM] * 9,
        out_specs=[VMEM] * 3,
        out_shape=[shape(TOK, COLS), shape(TOK, COLS), shape(TOK, STATE)],
        input_output_aliases={2: 0, 3: 1},
        scratch_shapes=[pltpu.VMEM((2, STATE, COLS), F32)],
        compiler_params=params(30),
        cost_estimate=cost(),
        name="mid_part",
    )(q, w, m, d, dq, zn, y2, y3, y23o)


def score_kernel(*refs):
    dq_in, zf_ref, zr_ref = refs[:3]
    pieces = refs[3:11]
    top_ref, low_ref, y = refs[11:]
    position, core, x, z0 = coords()
    for cr in range(2):
        for xr in range(4):
            piece = pieces[4 * cr + xr]
            place = ((cr ^ core) << 2) | (xr ^ x)
            rows = pl.ds(pl.multiple_of(place * 16, 16), 16)
            for index in range(2):
                pair = [piece[2 * z0 + index], piece[2 * (1 - z0) + index]]
                y[index, rows, :] = jnp.concatenate(pair, axis=0)
            y[2, rows, :] = piece[4:6].reshape(16, COLS)
    grads = dq_in[...]
    for block in BLOCKS:
        for index in range(3):
            z = zr_ref[0, :, block] if index == 2 else zf_ref[index, :, block]
            grads = grads + dot(z, y[index, :, block].astype(BF), 1, 1)
    top_ref[...] = grads[: TOK // 2]
    low_ref[...] = grads[TOK // 2 :]


def score_part(dq, zf, zr, pieces):
    part = shape(TOK // 2, STATE)
    return pl.pallas_call(
        score_kernel,
        in_specs=[VMEM] * 11,
        out_specs=[VMEM] * 3,
        out_shape=[part, part, shape(3, STATE, COLS)],
        compiler_params=params(20),
        cost_estimate=cost(),
        name="score_part",
    )(dq, zf, zr, *pieces)


def last_values_kernel(q_ref, d_in, y_ref, out_ref):
    position = lax.axis_index("seq")
    for block in BLOCKS:
        lower = None
        for index, k in enumerate((5, 6, 4)):
            part = (1 - ((position >> (k - 1)) & 1)).astype(F32) * y_ref[index, :, block]
            lower = part if lower is None else lower + part
        out_ref[:, block] = (d_in[:, block] + dot(q_ref[...], lower.astype(BF), 1, 0)).astype(BF)


def last_values(q, d, y):
    return pl.pallas_call(
        last_values_kernel,
        in_specs=[VMEM] * 3,
        out_specs=VMEM,
        out_shape=shape(TOK, COLS, kind=BF),
        compiler_params=params(20),
        cost_estimate=cost(),
        name="last_values",
    )(q, d, y)


def last_mixed_kernel(q_ref, w_ref, m_in, y_ref, out_ref):
    position = lax.axis_index("seq")
    for block in BLOCKS:
        outs = [dot(q_ref[...], y_ref[index, :, block].astype(BF), 1, 0) for index in range(3)]
        for a in range(SPANS):
            rows = slice(a * CH, (a + 1) * CH)
            total = m_in[rows, block]
            for index, k in enumerate((5, 6, 4)):
                upper = ((position >> (k - 1)) & 1).astype(F32)
                total = total + (upper * w_ref[k + 3, a : a + 1, block]) * outs[index][rows, :]
            out_ref[rows, block] = total.astype(BF)


def last_mixed(q, w, m, y):
    return pl.pallas_call(
        last_mixed_kernel,
        in_specs=[VMEM] * 4,
        out_specs=VMEM,
        out_shape=shape(TOK, COLS, kind=BF),
        compiler_params=params(20),
        cost_estimate=cost(),
        name="last_mixed",
    )(q, w, m, y)


def local(*args):
    tie = lax.optimization_barrier
    args = args[:3] + (args[3].transpose(1, 0, 2),) + args[4:]
    q_hbm, v_hbm, e_hbm, gain, code = [pltpu.with_memory_space_constraint(a, pltpu.HBM) for a in args]
    w, q, qt, v, e, zn, own_n, oth_n = near_states(code, gain, q_hbm, v_hbm, e_hbm)
    got_n = send(oth_n, 1)
    zf, own_f, oth_f = far_states(qt, v, e, w)
    near = [own_n[i] + got_n[i] for i in range(2)]
    near, own_f, oth_f = tie((near, own_f, oth_f))
    y2 = send(near[0], 2)
    y3 = send(near[1], 6)
    zr, own_f, oth_f, x1 = rest_states(qt, v, e, w, own_f, oth_f)
    got_f = send(oth_f, 1)
    y1 = send(x1, 1)

    chip = [own_f[j] + got_f[j] for j in range(4)]
    v2, chip, y1 = tie((v, chip, y1))
    slices = [send(chip[j], 2 * j) for j in (1, 2, 3)]
    m, d, dq = local_part(q, v2, e, w, zr, y1)
    slices, dq, near, y2, y3 = tie((slices, dq, near, y2, y3))
    y3b = send(near[1], 4)
    mine = [sum((s[i] for s in slices), chip[0][i]) for i in range(2)]
    other = sum((s[2:6] for s in slices), chip[0][2:6])

    low = send(other, 8)
    five = mine[0] + low[0]
    six = mine[1] + low[1]
    y5 = send(five, 16)
    y6 = send(six, 32) + send(six, 48)
    half = tie(jnp.stack([y5, y6]))
    rest = send(half, 8)
    quad = jnp.concatenate([half, rest, low[2:4]])
    quad, dq, y3b = tie((quad, dq, y3b))
    pieces = [quad] + [send(quad, 2 * j) for j in (1, 2, 3)]
    y3 = y3 + y3b
    y23o = send(jnp.stack([y2, y3]), 1)
    m, d, dq = mid_part(q, w, m, d, dq, zn, y2, y3, y23o)
    pieces[1], pieces[3], dq = tie((pieces[1], pieces[3], dq))
    swapped = [send(pieces[j], 1) for j in (0, 1, 3)]
    pieces[2], *swapped = tie((pieces[2], *swapped))
    swapped.insert(2, send(pieces[2], 1))
    pieces = pieces + swapped
    top, low, y = score_part(dq, zf, zr, pieces)
    got = [send(top, 1, "head"), send(low, 3, "head")]
    grad_values = last_values(q, d, y)
    got, grad_values = tie((got, grad_values))
    top = top + got[0]
    low = low + got[1]
    top, low, m = tie((top, low, m))
    got = [send(top, 3, "head"), send(low, 1, "head")]
    mixed = last_mixed(q, w, m, y)
    got, mixed = tie((got, mixed))
    grad_qk = jnp.concatenate([top + got[0], low + got[1]])
    return mixed, grad_qk, grad_values


def solution(mesh):
    placed = (P("seq", None), P("seq", "head"), P("seq", "head"), P(None, None, "head"), P("seq"))
    return jax.shard_map(
        local,
        mesh=mesh,
        in_specs=placed,
        out_specs=(P("seq", "head"), P("seq", None), P("seq", "head")),
        check_vma=False,
    )
```

```python
import functools

import jax
import jax.numpy as jnp
from jax import lax
from jax.experimental import pallas as pl
from jax.experimental.pallas import tpu as pltpu
from jax.sharding import PartitionSpec as P

HEAD_DIM = 64
CH = 64
TOK = 512
STATE = 128
COLS = 1280
HEADS = COLS // HEAD_DIM
BLK = 256
STEPS = COLS // BLK
SPANS = TOK // CH
USED = 10
TILE = 256
FIRST = 3
BF = jnp.bfloat16
F32 = jnp.float32
ROW, CORE, XMASK = 8, 1, 3
BLOCKS = tuple(slice(j * BLK, (j + 1) * BLK) for j in range(STEPS))

LOCAL = ((0, 0, 0), (0, 0, 1), (0, 0, 2), (1, 1, 0), (1, 1, 1), (1, 1, 2), (1, 0, 3))


def send(value, even, odd=None):
    odd = even if odd is None else odd
    pairs = [(source, source ^ (odd if source & CORE else even)) for source in range(lax.axis_size("seq"))]
    return lax.ppermute(value, "seq", pairs)


def send_head(value, even, odd):
    heads = lax.axis_size("head")
    pairs = []
    for source in range(lax.axis_size("seq")):
        for group in range(heads):
            target = group ^ (odd if source & CORE else even)
            pairs.append((source * heads + group, source * heads + target))
    return lax.ppermute(value, ("seq", "head"), pairs)


def neighbour(slot, core):
    return (slot * (1 + 2 * core)) & XMASK


def dot(a, b, over_a, over_b):
    return lax.dot_general(a, b, (((over_a,), (over_b,)), ((), ())), preferred_element_type=F32)


def coords():
    position = lax.axis_index("seq")
    return position, position & CORE, (position >> 1) & XMASK, (position >> 3) & CORE


def params(mib):
    return pltpu.CompilerParams(vmem_limit_bytes=mib * 1024 * 1024)


def cost():
    return pl.CostEstimate(flops=1024, bytes_accessed=1024, transcendentals=0)


def shape(*dims, kind=F32):
    return jax.ShapeDtypeStruct(dims, kind)


VMEM = pl.BlockSpec(memory_space=pltpu.VMEM)
SMEM = pl.BlockSpec(memory_space=pltpu.SMEM)
HBM = pl.BlockSpec(memory_space=pltpu.HBM)


def level_operand(z_ref, index, k, position, w_ref, v_ref, e_ref, block):
    upper = (position >> (k - 1)) & 1

    @pl.when(upper == 1)
    def _():
        for a in range(SPANS):
            rows = slice(a * CH, (a + 1) * CH)
            scaled = w_ref[k + 3, a : a + 1, block] * e_ref[rows, block].astype(F32)
            z_ref[index, rows, block] = scaled.astype(BF)

    @pl.when(upper == 0)
    def _():
        z_ref[index, :, block] = v_ref[:, block]


def far_kernel(
    code_hbm, gain_hbm, q_hbm, v_hbm, e_hbm, w_ref, q_ref, qt, v_ref, e_ref, z_ref, own_ref, oth_ref,
    code_ref, gain_ref, lw, res, sems
):
    position, core, x, z0 = coords()
    first = []
    for i, (far, near) in enumerate(((code_hbm, code_ref), (gain_hbm, gain_ref), (q_hbm, q_ref))):
        copy = pltpu.make_async_copy(far, near, sems.at[2 * STEPS + i])
        copy.start()
        first.append(copy)
    copies = []
    for j, block in enumerate(BLOCKS):
        for i, (far, near) in enumerate(((v_hbm, v_ref), (e_hbm, e_ref))):
            copy = pltpu.make_async_copy(far.at[:, block], near.at[:, block], sems.at[2 * j + i])
            copy.start()
            copies.append(copy)
    lw[...] = jnp.zeros_like(lw)
    for copy in first:
        copy.wait()
    for a in range(SPANS):
        lw[0:15, a : a + 1, 0:HEADS] = gain_ref[:, pl.ds(code_ref[a], 1), :]
    weights = lw[...].reshape(16 * SPANS, 128)[: USED * SPANS]
    high = weights.astype(BF)
    rest = weights - high.astype(F32)
    middle = rest.astype(BF)
    low = (rest - middle.astype(F32)).astype(BF)
    head = lax.broadcasted_iota(jnp.int32, (128, BLK), 0)
    for j, block in enumerate(BLOCKS):
        col = lax.broadcasted_iota(jnp.int32, (128, BLK), 1) + j * BLK
        spread = (head == col // HEAD_DIM).astype(BF)
        wide = dot(high, spread, 1, 0) + (dot(middle, spread, 1, 0) + dot(low, spread, 1, 0))
        w_ref[:, :, block] = wide.reshape(USED, SPANS, BLK)
    qt[...] = q_ref[...].T
    for j, block in enumerate(BLOCKS):
        copies[2 * j].wait()
        copies[2 * j + 1].wait()
        for index, k in enumerate((6, 4, 5)):
            level_operand(z_ref, index, k, position, w_ref, v_ref, e_ref, block)
            res[...] = dot(qt[...], z_ref[index, :, block], 1, 0).reshape(8, 2, ROW, BLK)
            for xr in range(4):
                for zr in range(2):
                    half = zr ^ z0 if k == 6 else zr
                    own_place = (core << 2) | (neighbour(xr, core) ^ x)
                    oth_place = ((core ^ 1) << 2) | (neighbour(xr, core ^ 1) ^ x)
                    own_ref[xr, 2 * index + zr, :, block] = res[own_place, half]
                    oth_ref[xr, 2 * index + zr, :, block] = res[oth_place, half]


def far_states(code, gain, q, v, e):
    return pl.pallas_call(
        far_kernel,
        in_specs=[HBM] * 5,
        out_specs=[VMEM] * 8,
        out_shape=[
            shape(USED, SPANS, COLS),
            shape(TOK, STATE, kind=BF),
            shape(STATE, TOK, kind=BF),
            shape(TOK, COLS, kind=BF),
            shape(TOK, COLS, kind=BF),
            shape(3, TOK, COLS, kind=BF),
            shape(4, 6, ROW, COLS),
            shape(4, 6, ROW, COLS),
        ],
        scratch_shapes=[
            pltpu.SMEM((SPANS,), jnp.int32),
            pltpu.VMEM((15, 16, HEADS), F32),
            pltpu.VMEM((16, SPANS, 128), F32),
            pltpu.VMEM((8, 2, ROW, BLK), F32),
            pltpu.SemaphoreType.DMA((2 * STEPS + 3,)),
        ],
        compiler_params=params(20),
        cost_estimate=cost(),
        name="far_states",
    )(code, gain, q, v, e)


def near_kernel(qt, v_ref, e_ref, w_ref, z_ref, x_ref, own_ref, oth_ref, res):
    position, core, x, z0 = coords()
    for index, k in enumerate((2, 3, 1)):
        for block in BLOCKS:
            level_operand(z_ref, index, k, position, w_ref, v_ref, e_ref, block)
            out = dot(qt[...], z_ref[index, :, block], 1, 0)
            if k == 1:
                x_ref[:, block] = out
            else:
                res[...] = out.reshape(2, STATE // 2, BLK)
                own_ref[index, :, block] = res[core]
                oth_ref[index, :, block] = res[core ^ 1]


def near_states(qt, v, e, w):
    half = STATE // 2
    return pl.pallas_call(
        near_kernel,
        in_specs=[VMEM] * 4,
        out_specs=[VMEM] * 4,
        out_shape=[
            shape(3, TOK, COLS, kind=BF),
            shape(STATE, COLS),
            shape(2, half, COLS),
            shape(2, half, COLS),
        ],
        scratch_shapes=[pltpu.VMEM((2, half, BLK), F32)],
        compiler_params=params(20),
        cost_estimate=cost(),
        name="near_states",
    )(qt, v, e, w)


def kept(level, flip):
    rows = lax.broadcasted_iota(jnp.int32, (TILE, TILE), 1 if flip else 0)
    keys = lax.broadcasted_iota(jnp.int32, (TILE, TILE), 0 if flip else 1)
    a, b = rows // CH, keys // CH
    if level == 0:
        return (a == b) & (keys <= rows)
    return ((a ^ b) >> (level - 1) == 1) & (a > b)


def add_outer(q_ref, w_ref, levels, position, y_ref, m_ref, d_ref, block):
    for index, k in enumerate(levels):

        @pl.when((position >> (k - 1)) & 1 == 1)
        def _():
            out = dot(q_ref[...], y_ref[index, :, block].astype(BF), 1, 0)
            for a in range(SPANS):
                rows = slice(a * CH, (a + 1) * CH)
                m_ref[rows, block] += w_ref[k + 3, a : a + 1, block] * out[rows, :]

    lower = None
    for index, k in enumerate(levels):
        part = (1 - ((position >> (k - 1)) & 1)).astype(F32) * y_ref[index, :, block]
        lower = part if lower is None else lower + part
    d_ref[:, block] += dot(q_ref[...], lower.astype(BF), 1, 0)


def local_blocks(first, count, q_ref, v_ref, e_ref, w_ref, score, flipped, m_ref, d_ref, dq_ref, grad, z):
    grad[...] = jnp.zeros_like(grad)
    per = TILE // CH

    def one_block(j, carry):
        block = pl.ds(pl.multiple_of((first + j) * BLK, BLK), BLK)
        out_block = pl.ds(pl.multiple_of(j * BLK, BLK), BLK)
        mixed = [None, None]
        d_val = [None, None]
        for index, (t, s, level) in enumerate(LOCAL):
            vals = v_ref[s * TILE : (s + 1) * TILE, block]
            for a in range(per):
                rows = slice(t * TILE + a * CH, t * TILE + (a + 1) * CH)
                w_row = w_ref[level, t * per + a : t * per + a + 1, block]
                z[index, a * CH : (a + 1) * CH, :] = (w_row * e_ref[rows, block].astype(F32)).astype(BF)
            out = dot(score[index], vals, 1, 0)
            w_rows = jnp.concatenate(
                [
                    jnp.broadcast_to(w_ref[level, t * per + a : t * per + a + 1, block], (CH, BLK))
                    for a in range(per)
                ],
                axis=0,
            )
            out = w_rows * out
            back = dot(flipped[index], z[index], 1, 0)
            mixed[t] = out if mixed[t] is None else mixed[t] + out
            d_val[s] = back if d_val[s] is None else d_val[s] + back
            grad[index] += dot(z[index], vals, 1, 1)
        for i in range(2):
            m_ref[i * TILE : (i + 1) * TILE, out_block] = mixed[i]
            d_ref[i * TILE : (i + 1) * TILE, out_block] = d_val[i]
        return carry

    lax.fori_loop(0, count, one_block, 0)
    q = [q_ref[i * TILE : (i + 1) * TILE, :] for i in range(2)]
    cross = grad[6].astype(BF)
    extra = [dot(cross, q[1], 0, 0), dot(cross, q[0], 1, 0)]
    for i in range(2):
        total = jnp.zeros((TILE, TILE), F32)
        for level in range(3):
            total = total + jnp.where(kept(level, False), grad[3 * i + level], 0.0)
        total = total.astype(BF)
        part = dot(total, q[i], 1, 0) + dot(total, q[i], 0, 0)
        dq_ref[i * TILE : (i + 1) * TILE, :] = part + extra[i]


def first_local_kernel(q_ref, v_ref, e_ref, w_ref, m_ref, d_ref, dq_ref, score, flipped, grad, z):
    for index, (t, s, level) in enumerate(LOCAL):
        qt_rows = q_ref[t * TILE : (t + 1) * TILE, :]
        qs_rows = q_ref[s * TILE : (s + 1) * TILE, :]
        direct = dot(qt_rows, qs_rows, 1, 1)
        swapped = dot(qs_rows, qt_rows, 1, 1)
        if level < 3:
            direct = jnp.where(kept(level, False), direct, 0.0)
            swapped = jnp.where(kept(level, True), swapped, 0.0)
        score[index] = direct.astype(BF)
        flipped[index] = swapped.astype(BF)
    local_blocks(0, FIRST, q_ref, v_ref, e_ref, w_ref, score, flipped, m_ref, d_ref, dq_ref, grad, z)


def other_local_kernel(q_ref, v_ref, e_ref, w_ref, score, flipped, m_ref, d_ref, dq_ref, grad, z):
    local_blocks(FIRST, STEPS - FIRST, q_ref, v_ref, e_ref, w_ref, score, flipped, m_ref, d_ref, dq_ref, grad, z)


def local_part(q, v, e, w, scores):
    wide = (STEPS - FIRST if scores else FIRST) * BLK
    kernel, name = (other_local_kernel, "other_local") if scores else (first_local_kernel, "first_local")
    table = shape(7, TILE, TILE, kind=BF)
    return pl.pallas_call(
        kernel,
        in_specs=[VMEM] * (4 + len(scores)),
        out_specs=[VMEM] * (5 - len(scores)),
        out_shape=[shape(TOK, wide), shape(TOK, wide), shape(TOK, STATE)] + [table] * (2 - len(scores)),
        scratch_shapes=[pltpu.VMEM((7, TILE, TILE), F32), pltpu.VMEM((7, TILE, BLK), BF)],
        compiler_params=params(20),
        cost_estimate=pl.CostEstimate(flops=1 << 33, bytes_accessed=1 << 25, transcendentals=0),
        name=name,
    )(q, v, e, w, *scores)


def mid_kernel(
    q_ref, w_ref, ma, da, dqa, mb, db, dqb, z_ref, y1_ref, y2_ref, y3_ref, y23o_ref, m_ref, d_ref, dq_ref, y
):
    position, core, x, z0 = coords()
    half = STATE // 2
    own = pl.ds(pl.multiple_of(core * half, half), half)
    oth = pl.ds(pl.multiple_of((core ^ 1) * half, half), half)
    for index, ref in enumerate((y2_ref, y3_ref)):
        y[index, own, :] = ref[...]
        y[index, oth, :] = y23o_ref[index]
    y[2] = y1_ref[...]
    grads = dqa[...] + dqb[...]
    m_ref[:, : FIRST * BLK] = ma[...]
    d_ref[:, : FIRST * BLK] = da[...]
    m_ref[:, FIRST * BLK :] = mb[...]
    d_ref[:, FIRST * BLK :] = db[...]
    for block in BLOCKS:
        add_outer(q_ref, w_ref, (2, 3, 1), position, y, m_ref, d_ref, block)
        for index in range(3):
            grads = grads + dot(z_ref[index, :, block], y[index, :, block].astype(BF), 1, 1)
    dq_ref[...] = grads


def mid_part(q, w, first, other, zn, y1, y2, y3, y23o):
    return pl.pallas_call(
        mid_kernel,
        in_specs=[VMEM] * 13,
        out_specs=[VMEM] * 3,
        out_shape=[shape(TOK, COLS), shape(TOK, COLS), shape(TOK, STATE)],
        scratch_shapes=[pltpu.VMEM((3, STATE, COLS), F32)],
        compiler_params=params(30),
        cost_estimate=cost(),
        name="mid_part",
    )(q, w, *first, *other, zn, y1, y2, y3, y23o)


def score_kernel(*refs):
    dq_in, zf_ref = refs[:2]
    pieces = refs[2:10]
    top_ref, low_ref, y = refs[10:]
    position, core, x, z0 = coords()
    for cr in range(2):
        for xr in range(4):
            piece = pieces[4 * cr + xr]
            place = ((cr ^ core) << 2) | (neighbour(xr, cr ^ core) ^ x)
            rows = pl.ds(pl.multiple_of(place * 16, 16), 16)
            y[0, rows, :] = jnp.concatenate([piece[z0], piece[1 - z0]], axis=0)
            y[1, rows, :] = piece[2:4].reshape(16, COLS)
            y[2, rows, :] = piece[4:6].reshape(16, COLS)
    grads = dq_in[...]
    for block in BLOCKS:
        for index in range(3):
            grads = grads + dot(zf_ref[index, :, block], y[index, :, block].astype(BF), 1, 1)
    top_ref[...] = grads[: TOK // 2]
    low_ref[...] = grads[TOK // 2 :]


def score_part(dq, zf, pieces):
    part = shape(TOK // 2, STATE)
    return pl.pallas_call(
        score_kernel,
        in_specs=[VMEM] * 10,
        out_specs=[VMEM] * 3,
        out_shape=[part, part, shape(3, STATE, COLS)],
        compiler_params=params(20),
        cost_estimate=cost(),
        name="score_part",
    )(dq, zf, *pieces)


def last_values_kernel(q_ref, d_in, y_ref, out_ref):
    position = lax.axis_index("seq")
    for block in BLOCKS:
        lower = None
        for index, k in enumerate((6, 4, 5)):
            part = (1 - ((position >> (k - 1)) & 1)).astype(F32) * y_ref[index, :, block]
            lower = part if lower is None else lower + part
        out_ref[:, block] = (d_in[:, block] + dot(q_ref[...], lower.astype(BF), 1, 0)).astype(BF)


def last_values(q, d, y):
    return pl.pallas_call(
        last_values_kernel,
        in_specs=[VMEM] * 3,
        out_specs=VMEM,
        out_shape=shape(TOK, COLS, kind=BF),
        compiler_params=params(20),
        cost_estimate=cost(),
        name="last_values",
    )(q, d, y)


def last_mixed_kernel(q_ref, w_ref, m_in, y_ref, out_ref):
    position = lax.axis_index("seq")
    for block in BLOCKS:
        outs = [dot(q_ref[...], y_ref[index, :, block].astype(BF), 1, 0) for index in range(3)]
        for a in range(SPANS):
            rows = slice(a * CH, (a + 1) * CH)
            total = m_in[rows, block]
            for index, k in enumerate((6, 4, 5)):
                upper = ((position >> (k - 1)) & 1).astype(F32)
                total = total + (upper * w_ref[k + 3, a : a + 1, block]) * outs[index][rows, :]
            out_ref[rows, block] = total.astype(BF)


def last_mixed(q, w, m, y):
    return pl.pallas_call(
        last_mixed_kernel,
        in_specs=[VMEM] * 4,
        out_specs=VMEM,
        out_shape=shape(TOK, COLS, kind=BF),
        compiler_params=params(20),
        cost_estimate=cost(),
        name="last_mixed",
    )(q, w, m, y)


def local(*args):
    tie = lax.optimization_barrier
    args = args[:3] + (args[3].transpose(1, 0, 2),) + args[4:]
    q_hbm, v_hbm, e_hbm, gain, code = [pltpu.with_memory_space_constraint(a, pltpu.HBM) for a in args]
    w, q, qt, v, e, zf, own_f, oth_f = far_states(code, gain, q_hbm, v_hbm, e_hbm)
    got_f = send(oth_f, 1)
    zn, x1, own_n, oth_n = near_states(qt, v, e, w)

    chip = [own_f[j] + got_f[j] for j in range(4)]
    chip, x1, oth_n = tie((chip, x1, oth_n))
    slices = [send(chip[j], 2 * j, 2 * (4 - j)) for j in (1, 2, 3)]
    got_n = send(oth_n, 1)
    y1 = send(x1, 1)
    near = [own_n[i] + got_n[i] for i in range(2)]
    slices, near, y1 = tie((slices, near, y1))
    mine = sum((s[0] for s in slices), chip[0][0])
    cross = sum((s[1:4] for s in slices), chip[0][1:4])
    pair = sum((s[4:6] for s in slices), chip[0][4:6])

    low = send(cross, 8)
    five = send(pair, 16)
    y2 = send(near[0], 2)
    y3 = [send(near[1], 6), send(near[1], 4)]
    six = mine + low[0]
    six, five, v2 = tie((six, five, v))
    y6 = [send(six, 32, 48), send(six, 48, 32)]
    *first, score, flipped = local_part(q, v2, e, w, ())
    half = jnp.concatenate([(y6[0] + y6[1])[None], five])
    half, score, v3 = tie((half, score, v2))
    rest = send(half, 8)
    other = local_part(q, v3, e, w, (score, flipped))
    rest, other = tie((rest, other))
    quad = jnp.concatenate([half[0:1], rest[0:1], low[1:3], half[1:3] + rest[1:3]])
    quad, other, y2, y3 = tie((quad, other, y2, y3))
    y3 = y3[0] + y3[1]
    y23o = send(jnp.stack([y2, y3]), 1)
    pieces = [quad] + [send(quad, 2 * j, 2 * (4 - j)) for j in (1, 2, 3)]
    m, d, dq = mid_part(q, w, first, other, zn, y1, y2, y3, y23o)
    for j in (1, 3, 2):
        pieces[j], dq = tie((pieces[j], dq))
    pieces = pieces + [send(p, 1) for p in pieces]
    top, low, y = score_part(dq, zf, pieces)
    got = [send_head(top, 1, 3), send_head(low, 3, 1)]
    grad_values = last_values(q, d, y)
    got, grad_values = tie((got, grad_values))
    top = top + got[0]
    low = low + got[1]
    top, low, m = tie((top, low, m))
    got = [send_head(top, 3, 1), send_head(low, 1, 3)]
    mixed = last_mixed(q, w, m, y)
    got, mixed = tie((got, mixed))
    grad_qk = jnp.concatenate([top + got[0], low + got[1]])
    return mixed, grad_qk, grad_values


def solution(mesh):
    placed = (P("seq", None), P("seq", "head"), P("seq", "head"), P(None, None, "head"), P("seq"))
    return jax.shard_map(
        local,
        mesh=mesh,
        in_specs=placed,
        out_specs=(P("seq", "head"), P("seq", None), P("seq", "head")),
        check_vma=False,
    )
```

```python
import functools

import jax
import jax.numpy as jnp
from jax import lax
from jax.experimental import pallas as pl
from jax.experimental.pallas import tpu as pltpu
from jax.sharding import PartitionSpec as P

HEAD_DIM = 64
CH = 64
TOK = 512
STATE = 128
COLS = 1280
HEADS = COLS // HEAD_DIM
BLK = 256
STEPS = COLS // BLK
SPANS = TOK // CH
USED = 10
TILE = 256
FIRST = 3
BF = jnp.bfloat16
F32 = jnp.float32
ROW, CORE, XMASK = 8, 1, 3
BLOCKS = tuple(slice(j * BLK, (j + 1) * BLK) for j in range(STEPS))

LOCAL = ((0, 0, 0), (0, 0, 1), (0, 0, 2), (1, 1, 0), (1, 1, 1), (1, 1, 2), (1, 0, 3))


def send(value, even, odd=None):
    odd = even if odd is None else odd
    pairs = [(source, source ^ (odd if source & CORE else even)) for source in range(lax.axis_size("seq"))]
    return lax.ppermute(value, "seq", pairs)


def send_head(value, even, odd):
    heads = lax.axis_size("head")
    pairs = []
    for source in range(lax.axis_size("seq")):
        for group in range(heads):
            target = group ^ (odd if source & CORE else even)
            pairs.append((source * heads + group, source * heads + target))
    return lax.ppermute(value, ("seq", "head"), pairs)


def neighbour(slot, core):
    return (slot * (1 + 2 * core)) & XMASK


def dot(a, b, over_a, over_b):
    return lax.dot_general(a, b, (((over_a,), (over_b,)), ((), ())), preferred_element_type=F32)


def coords():
    position = lax.axis_index("seq")
    return position, position & CORE, (position >> 1) & XMASK, (position >> 3) & CORE


def params(mib):
    return pltpu.CompilerParams(vmem_limit_bytes=mib * 1024 * 1024)


def cost():
    return pl.CostEstimate(flops=1024, bytes_accessed=1024, transcendentals=0)


def shape(*dims, kind=F32):
    return jax.ShapeDtypeStruct(dims, kind)


VMEM = pl.BlockSpec(memory_space=pltpu.VMEM)
SMEM = pl.BlockSpec(memory_space=pltpu.SMEM)
HBM = pl.BlockSpec(memory_space=pltpu.HBM)


def level_operand(z_ref, index, k, position, w_ref, v_ref, e_ref, block):
    upper = (position >> (k - 1)) & 1

    @pl.when(upper == 1)
    def _():
        for a in range(SPANS):
            rows = slice(a * CH, (a + 1) * CH)
            scaled = w_ref[k + 3, a : a + 1, block] * e_ref[rows, block].astype(F32)
            z_ref[index, rows, block] = scaled.astype(BF)

    @pl.when(upper == 0)
    def _():
        z_ref[index, :, block] = v_ref[:, block]


def far_kernel(
    code_hbm, gain_hbm, q_hbm, v_hbm, e_hbm, w_ref, q_ref, qt, v_ref, e_ref, z_ref, own_ref, oth_ref,
    code_ref, gain_ref, lw, res, sems
):
    position, core, x, z0 = coords()
    first = []
    for i, (far, near) in enumerate(((code_hbm, code_ref), (gain_hbm, gain_ref), (q_hbm, q_ref))):
        copy = pltpu.make_async_copy(far, near, sems.at[2 * STEPS + i])
        copy.start()
        first.append(copy)
    copies = []
    for j, block in enumerate(BLOCKS):
        for i, (far, near) in enumerate(((v_hbm, v_ref), (e_hbm, e_ref))):
            copy = pltpu.make_async_copy(far.at[:, block], near.at[:, block], sems.at[2 * j + i])
            copy.start()
            copies.append(copy)
    lw[...] = jnp.zeros_like(lw)
    for copy in first:
        copy.wait()
    for a in range(SPANS):
        lw[0:15, a : a + 1, 0:HEADS] = gain_ref[:, pl.ds(code_ref[a], 1), :]
    weights = lw[...].reshape(16 * SPANS, 128)[: USED * SPANS]
    high = weights.astype(BF)
    rest = weights - high.astype(F32)
    middle = rest.astype(BF)
    low = (rest - middle.astype(F32)).astype(BF)
    head = lax.broadcasted_iota(jnp.int32, (128, BLK), 0)
    for j, block in enumerate(BLOCKS):
        col = lax.broadcasted_iota(jnp.int32, (128, BLK), 1) + j * BLK
        spread = (head == col // HEAD_DIM).astype(BF)
        wide = dot(high, spread, 1, 0) + (dot(middle, spread, 1, 0) + dot(low, spread, 1, 0))
        w_ref[:, :, block] = wide.reshape(USED, SPANS, BLK)
    qt[...] = q_ref[...].T
    for j, block in enumerate(BLOCKS):
        copies[2 * j].wait()
        copies[2 * j + 1].wait()
        for index, k in enumerate((6, 4, 5)):
            level_operand(z_ref, index, k, position, w_ref, v_ref, e_ref, block)
            res[...] = dot(qt[...], z_ref[index, :, block], 1, 0).reshape(8, 2, ROW, BLK)
            for xr in range(4):
                for zr in range(2):
                    half = zr ^ z0 if k == 6 else zr
                    own_place = (core << 2) | (neighbour(xr, core) ^ x)
                    oth_place = ((core ^ 1) << 2) | (neighbour(xr, core ^ 1) ^ x)
                    own_ref[xr, 2 * index + zr, :, block] = res[own_place, half]
                    oth_ref[xr, 2 * index + zr, :, block] = res[oth_place, half]


def far_states(code, gain, q, v, e):
    return pl.pallas_call(
        far_kernel,
        in_specs=[HBM] * 5,
        out_specs=[VMEM] * 8,
        out_shape=[
            shape(USED, SPANS, COLS),
            shape(TOK, STATE, kind=BF),
            shape(STATE, TOK, kind=BF),
            shape(TOK, COLS, kind=BF),
            shape(TOK, COLS, kind=BF),
            shape(3, TOK, COLS, kind=BF),
            shape(4, 6, ROW, COLS),
            shape(4, 6, ROW, COLS),
        ],
        scratch_shapes=[
            pltpu.SMEM((SPANS,), jnp.int32),
            pltpu.VMEM((15, 16, HEADS), F32),
            pltpu.VMEM((16, SPANS, 128), F32),
            pltpu.VMEM((8, 2, ROW, BLK), F32),
            pltpu.SemaphoreType.DMA((2 * STEPS + 3,)),
        ],
        compiler_params=params(20),
        cost_estimate=cost(),
        name="far_states",
    )(code, gain, q, v, e)


def near_kernel(qt, v_ref, e_ref, w_ref, z_ref, x_ref, own_ref, oth_ref, res):
    position, core, x, z0 = coords()
    for index, k in enumerate((2, 3, 1)):
        for block in BLOCKS:
            level_operand(z_ref, index, k, position, w_ref, v_ref, e_ref, block)
            out = dot(qt[...], z_ref[index, :, block], 1, 0)
            if k == 1:
                x_ref[:, block] = out
            else:
                res[...] = out.reshape(2, STATE // 2, BLK)
                own_ref[index, :, block] = res[core]
                oth_ref[index, :, block] = res[core ^ 1]


def near_states(qt, v, e, w):
    half = STATE // 2
    return pl.pallas_call(
        near_kernel,
        in_specs=[VMEM] * 4,
        out_specs=[VMEM] * 4,
        out_shape=[
            shape(3, TOK, COLS, kind=BF),
            shape(STATE, COLS),
            shape(2, half, COLS),
            shape(2, half, COLS),
        ],
        scratch_shapes=[pltpu.VMEM((2, half, BLK), F32)],
        compiler_params=params(20),
        cost_estimate=cost(),
        name="near_states",
    )(qt, v, e, w)


def kept(level, flip):
    rows = lax.broadcasted_iota(jnp.int32, (TILE, TILE), 1 if flip else 0)
    keys = lax.broadcasted_iota(jnp.int32, (TILE, TILE), 0 if flip else 1)
    a, b = rows // CH, keys // CH
    if level == 0:
        return (a == b) & (keys <= rows)
    return ((a ^ b) >> (level - 1) == 1) & (a > b)


def add_outer(q_ref, w_ref, levels, position, y_ref, m_ref, d_ref, block):
    for index, k in enumerate(levels):

        @pl.when((position >> (k - 1)) & 1 == 1)
        def _():
            out = dot(q_ref[...], y_ref[index, :, block].astype(BF), 1, 0)
            for a in range(SPANS):
                rows = slice(a * CH, (a + 1) * CH)
                m_ref[rows, block] += w_ref[k + 3, a : a + 1, block] * out[rows, :]

    lower = None
    for index, k in enumerate(levels):
        part = (1 - ((position >> (k - 1)) & 1)).astype(F32) * y_ref[index, :, block]
        lower = part if lower is None else lower + part
    d_ref[:, block] += dot(q_ref[...], lower.astype(BF), 1, 0)


def local_blocks(first, count, v_ref, e_ref, w_ref, score, flipped, m_ref, d_ref, before, grad, z):
    per = TILE // CH

    def one_block(j, carry):
        block = pl.ds(pl.multiple_of((first + j) * BLK, BLK), BLK)
        out_block = pl.ds(pl.multiple_of(j * BLK, BLK), BLK)
        mixed = [None, None]
        d_val = [None, None]
        for index, (t, s, level) in enumerate(LOCAL):
            vals = v_ref[s * TILE : (s + 1) * TILE, block]
            for a in range(per):
                rows = slice(t * TILE + a * CH, t * TILE + (a + 1) * CH)
                w_row = w_ref[level, t * per + a : t * per + a + 1, block]
                z[index, a * CH : (a + 1) * CH, :] = (w_row * e_ref[rows, block].astype(F32)).astype(BF)
            out = dot(score[index], vals, 1, 0)
            w_rows = jnp.concatenate(
                [
                    jnp.broadcast_to(w_ref[level, t * per + a : t * per + a + 1, block], (CH, BLK))
                    for a in range(per)
                ],
                axis=0,
            )
            out = w_rows * out
            back = dot(flipped[index], z[index], 1, 0)
            mixed[t] = out if mixed[t] is None else mixed[t] + out
            d_val[s] = back if d_val[s] is None else d_val[s] + back
            grad[index] = before[index] + dot(z[index], vals, 1, 1)
        for i in range(2):
            m_ref[i * TILE : (i + 1) * TILE, out_block] = mixed[i]
            d_ref[i * TILE : (i + 1) * TILE, out_block] = d_val[i]
        return carry

    lax.fori_loop(0, count, one_block, 0)


def first_local_kernel(q_ref, v_ref, e_ref, w_ref, m_ref, d_ref, score, flipped, grad, z):
    grad[...] = jnp.zeros_like(grad)
    for index, (t, s, level) in enumerate(LOCAL):
        qt_rows = q_ref[t * TILE : (t + 1) * TILE, :]
        qs_rows = q_ref[s * TILE : (s + 1) * TILE, :]
        direct = dot(qt_rows, qs_rows, 1, 1)
        swapped = dot(qs_rows, qt_rows, 1, 1)
        if level < 3:
            direct = jnp.where(kept(level, False), direct, 0.0)
            swapped = jnp.where(kept(level, True), swapped, 0.0)
        score[index] = direct.astype(BF)
        flipped[index] = swapped.astype(BF)
    local_blocks(0, FIRST, v_ref, e_ref, w_ref, score, flipped, m_ref, d_ref, grad, grad, z)


def next_local_kernel(q_ref, v_ref, e_ref, w_ref, score, flipped, before, m_ref, d_ref, grad, z):
    local_blocks(FIRST, 1, v_ref, e_ref, w_ref, score, flipped, m_ref, d_ref, before, grad, z)


def end_local_kernel(q_ref, v_ref, e_ref, w_ref, score, flipped, before, m_ref, d_ref, dq_ref, grad, z):
    local_blocks(FIRST + 1, 1, v_ref, e_ref, w_ref, score, flipped, m_ref, d_ref, before, grad, z)
    q = [q_ref[i * TILE : (i + 1) * TILE, :] for i in range(2)]
    cross = grad[6].astype(BF)
    extra = [dot(cross, q[1], 0, 0), dot(cross, q[0], 1, 0)]
    for i in range(2):
        total = jnp.zeros((TILE, TILE), F32)
        for level in range(3):
            total = total + jnp.where(kept(level, False), grad[3 * i + level], 0.0)
        total = total.astype(BF)
        part = dot(total, q[i], 1, 0) + dot(total, q[i], 0, 0)
        dq_ref[i * TILE : (i + 1) * TILE, :] = part + extra[i]


def local_part(stage, q, v, e, w, tables):
    kernel = (first_local_kernel, next_local_kernel, end_local_kernel)[stage]
    wide = BLK if stage else FIRST * BLK
    table = shape(7, TILE, TILE, kind=BF)
    grad = shape(7, TILE, TILE)
    outs = ([table, table, grad], [grad], [shape(TOK, STATE)])[stage]
    scratch = [pltpu.VMEM((7, TILE, BLK), BF)]
    if stage == 2:
        scratch = [pltpu.VMEM((7, TILE, TILE), F32)] + scratch
    return pl.pallas_call(
        kernel,
        in_specs=[VMEM] * (4 + len(tables)),
        out_specs=[VMEM] * (2 + len(outs)),
        out_shape=[shape(TOK, wide), shape(TOK, wide)] + outs,
        scratch_shapes=scratch,
        compiler_params=params(20),
        cost_estimate=pl.CostEstimate(flops=1 << 33, bytes_accessed=1 << 25, transcendentals=0),
        name=("first_local", "next_local", "end_local")[stage],
    )(q, v, e, w, *tables)


def mid_kernel(
    q_ref, w_ref, ma, da, mb, db, mc, dc, dq_in, z_ref, y1_ref, y2_ref, y3_ref, y23o_ref, m_ref, d_ref, dq_ref, y
):
    position, core, x, z0 = coords()
    half = STATE // 2
    own = pl.ds(pl.multiple_of(core * half, half), half)
    oth = pl.ds(pl.multiple_of((core ^ 1) * half, half), half)
    for index, ref in enumerate((y2_ref, y3_ref)):
        y[index, own, :] = ref[...]
        y[index, oth, :] = y23o_ref[index]
    y[2] = y1_ref[...]
    grads = dq_in[...]
    m_ref[:, : FIRST * BLK] = ma[...]
    d_ref[:, : FIRST * BLK] = da[...]
    m_ref[:, BLOCKS[FIRST]] = mb[...]
    d_ref[:, BLOCKS[FIRST]] = db[...]
    m_ref[:, BLOCKS[FIRST + 1]] = mc[...]
    d_ref[:, BLOCKS[FIRST + 1]] = dc[...]
    for block in BLOCKS:
        add_outer(q_ref, w_ref, (2, 3, 1), position, y, m_ref, d_ref, block)
        for index in range(3):
            grads = grads + dot(z_ref[index, :, block], y[index, :, block].astype(BF), 1, 1)
    dq_ref[...] = grads


def mid_part(q, w, own, zn, y1, y2, y3, y23o):
    return pl.pallas_call(
        mid_kernel,
        in_specs=[VMEM] * 14,
        out_specs=[VMEM] * 3,
        out_shape=[shape(TOK, COLS), shape(TOK, COLS), shape(TOK, STATE)],
        scratch_shapes=[pltpu.VMEM((3, STATE, COLS), F32)],
        compiler_params=params(30),
        cost_estimate=cost(),
        name="mid_part",
    )(q, w, *own, zn, y1, y2, y3, y23o)


def score_kernel(*refs):
    dq_in, zf_ref = refs[:2]
    pieces = refs[2:10]
    top_ref, low_ref, y = refs[10:]
    position, core, x, z0 = coords()
    for cr in range(2):
        for xr in range(4):
            piece = pieces[4 * cr + xr]
            place = ((cr ^ core) << 2) | (neighbour(xr, cr ^ core) ^ x)
            rows = pl.ds(pl.multiple_of(place * 16, 16), 16)
            y[0, rows, :] = jnp.concatenate([piece[z0], piece[1 - z0]], axis=0)
            y[1, rows, :] = piece[2:4].reshape(16, COLS)
            y[2, rows, :] = piece[4:6].reshape(16, COLS)
    grads = dq_in[...]
    for block in BLOCKS:
        for index in range(3):
            grads = grads + dot(zf_ref[index, :, block], y[index, :, block].astype(BF), 1, 1)
    top_ref[...] = grads[: TOK // 2]
    low_ref[...] = grads[TOK // 2 :]


def score_part(dq, zf, pieces):
    part = shape(TOK // 2, STATE)
    return pl.pallas_call(
        score_kernel,
        in_specs=[VMEM] * 10,
        out_specs=[VMEM] * 3,
        out_shape=[part, part, shape(3, STATE, COLS)],
        compiler_params=params(20),
        cost_estimate=cost(),
        name="score_part",
    )(dq, zf, *pieces)


def last_values_kernel(q_ref, d_in, y_ref, out_ref):
    position = lax.axis_index("seq")
    for block in BLOCKS:
        lower = None
        for index, k in enumerate((6, 4, 5)):
            part = (1 - ((position >> (k - 1)) & 1)).astype(F32) * y_ref[index, :, block]
            lower = part if lower is None else lower + part
        out_ref[:, block] = (d_in[:, block] + dot(q_ref[...], lower.astype(BF), 1, 0)).astype(BF)


def last_values(q, d, y):
    return pl.pallas_call(
        last_values_kernel,
        in_specs=[VMEM] * 3,
        out_specs=VMEM,
        out_shape=shape(TOK, COLS, kind=BF),
        compiler_params=params(20),
        cost_estimate=cost(),
        name="last_values",
    )(q, d, y)


def last_mixed_kernel(q_ref, w_ref, m_in, y_ref, out_ref):
    position = lax.axis_index("seq")
    for block in BLOCKS:
        outs = [dot(q_ref[...], y_ref[index, :, block].astype(BF), 1, 0) for index in range(3)]
        for a in range(SPANS):
            rows = slice(a * CH, (a + 1) * CH)
            total = m_in[rows, block]
            for index, k in enumerate((6, 4, 5)):
                upper = ((position >> (k - 1)) & 1).astype(F32)
                total = total + (upper * w_ref[k + 3, a : a + 1, block]) * outs[index][rows, :]
            out_ref[rows, block] = total.astype(BF)


def last_mixed(q, w, m, y):
    return pl.pallas_call(
        last_mixed_kernel,
        in_specs=[VMEM] * 4,
        out_specs=VMEM,
        out_shape=shape(TOK, COLS, kind=BF),
        compiler_params=params(20),
        cost_estimate=cost(),
        name="last_mixed",
    )(q, w, m, y)


def local(*args):
    tie = lax.optimization_barrier
    args = args[:3] + (args[3].transpose(1, 0, 2),) + args[4:]
    q_hbm, v_hbm, e_hbm, gain, code = [pltpu.with_memory_space_constraint(a, pltpu.HBM) for a in args]
    w, q, qt, v, e, zf, own_f, oth_f = far_states(code, gain, q_hbm, v_hbm, e_hbm)
    got_f = send(oth_f, 1)
    zn, x1, own_n, oth_n = near_states(qt, v, e, w)

    chip = [own_f[j] + got_f[j] for j in range(4)]
    chip, x1, oth_n, v1 = tie((chip, x1, oth_n, v))
    slices = [send(chip[j], 2 * j, 2 * (4 - j)) for j in (1, 2, 3)]
    got_n = send(oth_n, 1)
    y1 = send(x1, 1)
    near = [own_n[i] + got_n[i] for i in range(2)]
    ma, da, score, flipped, grad = local_part(0, q, v1, e, w, ())
    slices, near, y1, grad = tie((slices, near, y1, grad))
    mine = sum((s[0] for s in slices), chip[0][0])
    cross = sum((s[1:4] for s in slices), chip[0][1:4])
    pair = sum((s[4:6] for s in slices), chip[0][4:6])

    low = send(cross, 8)
    five = send(pair, 16)
    y2 = send(near[0], 2)
    y3 = [send(near[1], 6), send(near[1], 4)]
    low, five = tie((low, five))
    six = mine + low[0]
    six, v2 = tie((six, v1))
    y6 = [send(six, 32, 48), send(six, 48, 32)]
    mb, db, grad = local_part(1, q, v2, e, w, (score, flipped, grad))
    half = jnp.concatenate([(y6[0] + y6[1])[None], five])
    half, grad, v3 = tie((half, grad, v2))
    rest = send(half, 8)
    mc, dc, dq = local_part(2, q, v3, e, w, (score, flipped, grad))
    rest, dq = tie((rest, dq))
    quad = jnp.concatenate([half[0:1], rest[0:1], low[1:3], half[1:3] + rest[1:3]])
    quad, dq, y2, y3 = tie((quad, dq, y2, y3))
    y3 = y3[0] + y3[1]
    y23o = send(jnp.stack([y2, y3]), 1)
    pieces = [quad] + [send(quad, 2 * j, 2 * (4 - j)) for j in (1, 2, 3)]
    m, d, dq = mid_part(q, w, (ma, da, mb, db, mc, dc, dq), zn, y1, y2, y3, y23o)
    for j in (1, 3, 2):
        pieces[j], dq = tie((pieces[j], dq))
    pieces = pieces + [send(p, 1) for p in pieces]
    top, low, y = score_part(dq, zf, pieces)
    got = [send_head(top, 1, 3), send_head(low, 3, 1)]
    grad_values = last_values(q, d, y)
    got, grad_values = tie((got, grad_values))
    top = top + got[0]
    low = low + got[1]
    top, low, m = tie((top, low, m))
    got = [send_head(top, 3, 1), send_head(low, 1, 3)]
    mixed = last_mixed(q, w, m, y)
    got, mixed = tie((got, mixed))
    grad_qk = jnp.concatenate([top + got[0], low + got[1]])
    return mixed, grad_qk, grad_values


def solution(mesh):
    placed = (P("seq", None), P("seq", "head"), P("seq", "head"), P(None, None, "head"), P("seq"))
    return jax.shard_map(
        local,
        mesh=mesh,
        in_specs=placed,
        out_specs=(P("seq", "head"), P("seq", None), P("seq", "head")),
        check_vma=False,
    )
```

```python
import functools

import jax
import jax.numpy as jnp
from jax import lax
from jax.experimental import pallas as pl
from jax.experimental.pallas import tpu as pltpu
from jax.sharding import PartitionSpec as P

HEAD_DIM = 64
CH = 64
TOK = 512
STATE = 128
COLS = 1280
HEADS = COLS // HEAD_DIM
BLK = 256
STEPS = COLS // BLK
SPANS = TOK // CH
USED = 10
TILE = 256
FIRST = 3
BF = jnp.bfloat16
F32 = jnp.float32
ROW, CORE, XMASK = 8, 1, 3
BLOCKS = tuple(slice(j * BLK, (j + 1) * BLK) for j in range(STEPS))

LOCAL = ((0, 0, 0), (0, 0, 1), (0, 0, 2), (1, 1, 0), (1, 1, 1), (1, 1, 2), (1, 0, 3))


def send(value, even, odd=None):
    odd = even if odd is None else odd
    pairs = [(source, source ^ (odd if source & CORE else even)) for source in range(lax.axis_size("seq"))]
    return lax.ppermute(value, "seq", pairs)


def send_head(value, even, odd):
    heads = lax.axis_size("head")
    pairs = []
    for source in range(lax.axis_size("seq")):
        for group in range(heads):
            target = group ^ (odd if source & CORE else even)
            pairs.append((source * heads + group, source * heads + target))
    return lax.ppermute(value, ("seq", "head"), pairs)


def neighbour(slot, core):
    return (slot * (1 + 2 * core)) & XMASK


def dot(a, b, over_a, over_b):
    return lax.dot_general(a, b, (((over_a,), (over_b,)), ((), ())), preferred_element_type=F32)


def coords():
    position = lax.axis_index("seq")
    return position, position & CORE, (position >> 1) & XMASK, (position >> 3) & CORE


def params(mib):
    return pltpu.CompilerParams(vmem_limit_bytes=mib * 1024 * 1024)


def cost():
    return pl.CostEstimate(flops=1024, bytes_accessed=1024, transcendentals=0)


def shape(*dims, kind=F32):
    return jax.ShapeDtypeStruct(dims, kind)


VMEM = pl.BlockSpec(memory_space=pltpu.VMEM)
SMEM = pl.BlockSpec(memory_space=pltpu.SMEM)
HBM = pl.BlockSpec(memory_space=pltpu.HBM)


def level_operand(z_ref, index, k, position, w_ref, v_ref, e_ref, block):
    upper = (position >> (k - 1)) & 1

    @pl.when(upper == 1)
    def _():
        for a in range(SPANS):
            rows = slice(a * CH, (a + 1) * CH)
            scaled = w_ref[k + 3, a : a + 1, block] * e_ref[rows, block].astype(F32)
            z_ref[index, rows, block] = scaled.astype(BF)

    @pl.when(upper == 0)
    def _():
        z_ref[index, :, block] = v_ref[:, block]


def far_kernel(
    code_hbm, gain_hbm, q_hbm, v_hbm, e_hbm, w_ref, q_ref, qt, v_ref, e_ref, z_ref, own_ref, oth_ref,
    code_ref, gain_ref, lw, res, sems
):
    position, core, x, z0 = coords()
    first = []
    for i, (far, near) in enumerate(((code_hbm, code_ref), (gain_hbm, gain_ref), (q_hbm, q_ref))):
        copy = pltpu.make_async_copy(far, near, sems.at[2 * STEPS + i])
        copy.start()
        first.append(copy)
    copies = []
    for j, block in enumerate(BLOCKS):
        for i, (far, near) in enumerate(((v_hbm, v_ref), (e_hbm, e_ref))):
            copy = pltpu.make_async_copy(far.at[:, block], near.at[:, block], sems.at[2 * j + i])
            copy.start()
            copies.append(copy)
    lw[...] = jnp.zeros_like(lw)
    for copy in first:
        copy.wait()
    for a in range(SPANS):
        lw[0:15, a : a + 1, 0:HEADS] = gain_ref[:, pl.ds(code_ref[a], 1), :]
    weights = lw[...].reshape(16 * SPANS, 128)[: USED * SPANS]
    high = weights.astype(BF)
    rest = weights - high.astype(F32)
    middle = rest.astype(BF)
    low = (rest - middle.astype(F32)).astype(BF)
    head = lax.broadcasted_iota(jnp.int32, (128, BLK), 0)
    for j, block in enumerate(BLOCKS):
        col = lax.broadcasted_iota(jnp.int32, (128, BLK), 1) + j * BLK
        spread = (head == col // HEAD_DIM).astype(BF)
        wide = dot(high, spread, 1, 0) + (dot(middle, spread, 1, 0) + dot(low, spread, 1, 0))
        w_ref[:, :, block] = wide.reshape(USED, SPANS, BLK)
    qt[...] = q_ref[...].T
    for j, block in enumerate(BLOCKS):
        copies[2 * j].wait()
        copies[2 * j + 1].wait()
        for index, k in enumerate((6, 4, 5)):
            level_operand(z_ref, index, k, position, w_ref, v_ref, e_ref, block)
            res[...] = dot(qt[...], z_ref[index, :, block], 1, 0).reshape(8, 2, ROW, BLK)
            for xr in range(4):
                for zr in range(2):
                    half = zr ^ z0 if k == 6 else zr
                    own_place = (core << 2) | (neighbour(xr, core) ^ x)
                    oth_place = ((core ^ 1) << 2) | (neighbour(xr, core ^ 1) ^ x)
                    own_ref[xr, 2 * index + zr, :, block] = res[own_place, half]
                    oth_ref[xr, 2 * index + zr, :, block] = res[oth_place, half]


def far_states(code, gain, q, v, e):
    return pl.pallas_call(
        far_kernel,
        in_specs=[HBM] * 5,
        out_specs=[VMEM] * 8,
        out_shape=[
            shape(USED, SPANS, COLS),
            shape(TOK, STATE, kind=BF),
            shape(STATE, TOK, kind=BF),
            shape(TOK, COLS, kind=BF),
            shape(TOK, COLS, kind=BF),
            shape(3, TOK, COLS, kind=BF),
            shape(4, 6, ROW, COLS),
            shape(4, 6, ROW, COLS),
        ],
        scratch_shapes=[
            pltpu.SMEM((SPANS,), jnp.int32),
            pltpu.VMEM((15, 16, HEADS), F32),
            pltpu.VMEM((16, SPANS, 128), F32),
            pltpu.VMEM((8, 2, ROW, BLK), F32),
            pltpu.SemaphoreType.DMA((2 * STEPS + 3,)),
        ],
        compiler_params=params(20),
        cost_estimate=cost(),
        name="far_states",
    )(code, gain, q, v, e)


def near_kernel(qt, v_ref, e_ref, w_ref, z_ref, own_ref, oth_ref, res):
    position, core, x, z0 = coords()
    for index, k in enumerate((2, 3)):
        for block in BLOCKS:
            level_operand(z_ref, index, k, position, w_ref, v_ref, e_ref, block)
            res[...] = dot(qt[...], z_ref[index, :, block], 1, 0).reshape(2, STATE // 2, BLK)
            own_ref[index, :, block] = res[core]
            oth_ref[index, :, block] = res[core ^ 1]


def near_states(qt, v, e, w):
    half = STATE // 2
    return pl.pallas_call(
        near_kernel,
        in_specs=[VMEM] * 4,
        out_specs=[VMEM] * 3,
        out_shape=[
            shape(2, TOK, COLS, kind=BF),
            shape(2, half, COLS),
            shape(2, half, COLS),
        ],
        scratch_shapes=[pltpu.VMEM((2, half, BLK), F32)],
        compiler_params=params(20),
        cost_estimate=cost(),
        name="near_states",
    )(qt, v, e, w)


def kept(level, flip):
    rows = lax.broadcasted_iota(jnp.int32, (TILE, TILE), 1 if flip else 0)
    keys = lax.broadcasted_iota(jnp.int32, (TILE, TILE), 0 if flip else 1)
    a, b = rows // CH, keys // CH
    if level == 0:
        return (a == b) & (keys <= rows)
    return ((a ^ b) >> (level - 1) == 1) & (a > b)


def add_outer(q_ref, w_ref, levels, position, y_ref, m_ref, d_ref, block):
    for index, k in enumerate(levels):

        @pl.when((position >> (k - 1)) & 1 == 1)
        def _():
            out = dot(q_ref[...], y_ref[index, :, block].astype(BF), 1, 0)
            for a in range(SPANS):
                rows = slice(a * CH, (a + 1) * CH)
                m_ref[rows, block] += w_ref[k + 3, a : a + 1, block] * out[rows, :]

    lower = None
    for index, k in enumerate(levels):
        part = (1 - ((position >> (k - 1)) & 1)).astype(F32) * y_ref[index, :, block]
        lower = part if lower is None else lower + part
    d_ref[:, block] += dot(q_ref[...], lower.astype(BF), 1, 0)


def local_blocks(first, count, v_ref, e_ref, w_ref, score, flipped, m_ref, d_ref, before, grad, z):
    per = TILE // CH

    def one_block(j, carry):
        block = pl.ds(pl.multiple_of((first + j) * BLK, BLK), BLK)
        out_block = pl.ds(pl.multiple_of(j * BLK, BLK), BLK)
        mixed = [None, None]
        d_val = [None, None]
        for index, (t, s, level) in enumerate(LOCAL):
            vals = v_ref[s * TILE : (s + 1) * TILE, block]
            for a in range(per):
                rows = slice(t * TILE + a * CH, t * TILE + (a + 1) * CH)
                w_row = w_ref[level, t * per + a : t * per + a + 1, block]
                z[index, a * CH : (a + 1) * CH, :] = (w_row * e_ref[rows, block].astype(F32)).astype(BF)
            out = dot(score[index], vals, 1, 0)
            w_rows = jnp.concatenate(
                [
                    jnp.broadcast_to(w_ref[level, t * per + a : t * per + a + 1, block], (CH, BLK))
                    for a in range(per)
                ],
                axis=0,
            )
            out = w_rows * out
            back = dot(flipped[index], z[index], 1, 0)
            mixed[t] = out if mixed[t] is None else mixed[t] + out
            d_val[s] = back if d_val[s] is None else d_val[s] + back
            grad[index] = before[index] + dot(z[index], vals, 1, 1)
        for i in range(2):
            m_ref[i * TILE : (i + 1) * TILE, out_block] = mixed[i]
            d_ref[i * TILE : (i + 1) * TILE, out_block] = d_val[i]
        return carry

    lax.fori_loop(0, count, one_block, 0)


def first_local_kernel(
    q_ref, v_ref, e_ref, w_ref, qt, m_ref, d_ref, score, flipped, grad, z1_ref, x1_ref, z
):
    position = lax.axis_index("seq")
    for block in BLOCKS:
        level_operand(z1_ref, 0, 1, position, w_ref, v_ref, e_ref, block)
        x1_ref[:, block] = dot(qt[...], z1_ref[0, :, block], 1, 0)
    grad[...] = jnp.zeros_like(grad)
    for index, (t, s, level) in enumerate(LOCAL):
        qt_rows = q_ref[t * TILE : (t + 1) * TILE, :]
        qs_rows = q_ref[s * TILE : (s + 1) * TILE, :]
        direct = dot(qt_rows, qs_rows, 1, 1)
        swapped = dot(qs_rows, qt_rows, 1, 1)
        if level < 3:
            direct = jnp.where(kept(level, False), direct, 0.0)
            swapped = jnp.where(kept(level, True), swapped, 0.0)
        score[index] = direct.astype(BF)
        flipped[index] = swapped.astype(BF)
    local_blocks(0, FIRST, v_ref, e_ref, w_ref, score, flipped, m_ref, d_ref, grad, grad, z)


def next_local_kernel(q_ref, v_ref, e_ref, w_ref, score, flipped, before, m_ref, d_ref, grad, z):
    local_blocks(FIRST, 1, v_ref, e_ref, w_ref, score, flipped, m_ref, d_ref, before, grad, z)


def end_local_kernel(q_ref, v_ref, e_ref, w_ref, score, flipped, before, m_ref, d_ref, dq_ref, grad, z):
    local_blocks(FIRST + 1, 1, v_ref, e_ref, w_ref, score, flipped, m_ref, d_ref, before, grad, z)
    q = [q_ref[i * TILE : (i + 1) * TILE, :] for i in range(2)]
    cross = grad[6].astype(BF)
    extra = [dot(cross, q[1], 0, 0), dot(cross, q[0], 1, 0)]
    for i in range(2):
        total = jnp.zeros((TILE, TILE), F32)
        for level in range(3):
            total = total + jnp.where(kept(level, False), grad[3 * i + level], 0.0)
        total = total.astype(BF)
        part = dot(total, q[i], 1, 0) + dot(total, q[i], 0, 0)
        dq_ref[i * TILE : (i + 1) * TILE, :] = part + extra[i]


def local_part(stage, q, v, e, w, tables):
    kernel = (first_local_kernel, next_local_kernel, end_local_kernel)[stage]
    wide = BLK if stage else FIRST * BLK
    table = shape(7, TILE, TILE, kind=BF)
    grad = shape(7, TILE, TILE)
    level_one = [shape(1, TOK, COLS, kind=BF), shape(STATE, COLS)]
    outs = ([table, table, grad] + level_one, [grad], [shape(TOK, STATE)])[stage]
    scratch = [pltpu.VMEM((7, TILE, BLK), BF)]
    if stage == 2:
        scratch = [pltpu.VMEM((7, TILE, TILE), F32)] + scratch
    return pl.pallas_call(
        kernel,
        in_specs=[VMEM] * (4 + len(tables)),
        out_specs=[VMEM] * (2 + len(outs)),
        out_shape=[shape(TOK, wide), shape(TOK, wide)] + outs,
        scratch_shapes=scratch,
        compiler_params=params(20),
        cost_estimate=pl.CostEstimate(flops=1 << 33, bytes_accessed=1 << 25, transcendentals=0),
        name=("first_local", "next_local", "end_local")[stage],
    )(q, v, e, w, *tables)


def mid_kernel(
    q_ref, w_ref, ma, da, mb, db, mc, dc, dq_in, z_ref, z1_ref, y1_ref, y2_ref, y3_ref, y23o_ref, m_ref, d_ref, dq_ref, y
):
    position, core, x, z0 = coords()
    half = STATE // 2
    own = pl.ds(pl.multiple_of(core * half, half), half)
    oth = pl.ds(pl.multiple_of((core ^ 1) * half, half), half)
    for index, ref in enumerate((y2_ref, y3_ref)):
        y[index, own, :] = ref[...]
        y[index, oth, :] = y23o_ref[index]
    y[2] = y1_ref[...]
    grads = dq_in[...]
    m_ref[:, : FIRST * BLK] = ma[...]
    d_ref[:, : FIRST * BLK] = da[...]
    m_ref[:, BLOCKS[FIRST]] = mb[...]
    d_ref[:, BLOCKS[FIRST]] = db[...]
    m_ref[:, BLOCKS[FIRST + 1]] = mc[...]
    d_ref[:, BLOCKS[FIRST + 1]] = dc[...]
    for block in BLOCKS:
        add_outer(q_ref, w_ref, (2, 3, 1), position, y, m_ref, d_ref, block)
        for index in range(3):
            z = z1_ref[0, :, block] if index == 2 else z_ref[index, :, block]
            grads = grads + dot(z, y[index, :, block].astype(BF), 1, 1)
    dq_ref[...] = grads


def mid_part(q, w, own, zn, z1, y1, y2, y3, y23o):
    return pl.pallas_call(
        mid_kernel,
        in_specs=[VMEM] * 15,
        out_specs=[VMEM] * 3,
        out_shape=[shape(TOK, COLS), shape(TOK, COLS), shape(TOK, STATE)],
        scratch_shapes=[pltpu.VMEM((3, STATE, COLS), F32)],
        compiler_params=params(30),
        cost_estimate=cost(),
        name="mid_part",
    )(q, w, *own, zn, z1, y1, y2, y3, y23o)


def score_kernel(*refs):
    dq_in, zf_ref = refs[:2]
    pieces = refs[2:10]
    top_ref, low_ref, y = refs[10:]
    position, core, x, z0 = coords()
    for cr in range(2):
        for xr in range(4):
            piece = pieces[4 * cr + xr]
            place = ((cr ^ core) << 2) | (neighbour(xr, cr ^ core) ^ x)
            rows = pl.ds(pl.multiple_of(place * 16, 16), 16)
            y[0, rows, :] = jnp.concatenate([piece[z0], piece[1 - z0]], axis=0)
            y[1, rows, :] = piece[2:4].reshape(16, COLS)
            y[2, rows, :] = piece[4:6].reshape(16, COLS)
    grads = dq_in[...]
    for block in BLOCKS:
        for index in range(3):
            grads = grads + dot(zf_ref[index, :, block], y[index, :, block].astype(BF), 1, 1)
    top_ref[...] = grads[: TOK // 2]
    low_ref[...] = grads[TOK // 2 :]


def score_part(dq, zf, pieces):
    part = shape(TOK // 2, STATE)
    return pl.pallas_call(
        score_kernel,
        in_specs=[VMEM] * 10,
        out_specs=[VMEM] * 3,
        out_shape=[part, part, shape(3, STATE, COLS)],
        compiler_params=params(20),
        cost_estimate=cost(),
        name="score_part",
    )(dq, zf, *pieces)


def last_values_kernel(q_ref, d_in, y_ref, out_ref):
    position = lax.axis_index("seq")
    for block in BLOCKS:
        lower = None
        for index, k in enumerate((6, 4, 5)):
            part = (1 - ((position >> (k - 1)) & 1)).astype(F32) * y_ref[index, :, block]
            lower = part if lower is None else lower + part
        out_ref[:, block] = (d_in[:, block] + dot(q_ref[...], lower.astype(BF), 1, 0)).astype(BF)


def last_values(q, d, y):
    return pl.pallas_call(
        last_values_kernel,
        in_specs=[VMEM] * 3,
        out_specs=VMEM,
        out_shape=shape(TOK, COLS, kind=BF),
        compiler_params=params(20),
        cost_estimate=cost(),
        name="last_values",
    )(q, d, y)


def last_mixed_kernel(q_ref, w_ref, m_in, y_ref, out_ref):
    position = lax.axis_index("seq")
    for block in BLOCKS:
        outs = [dot(q_ref[...], y_ref[index, :, block].astype(BF), 1, 0) for index in range(3)]
        for a in range(SPANS):
            rows = slice(a * CH, (a + 1) * CH)
            total = m_in[rows, block]
            for index, k in enumerate((6, 4, 5)):
                upper = ((position >> (k - 1)) & 1).astype(F32)
                total = total + (upper * w_ref[k + 3, a : a + 1, block]) * outs[index][rows, :]
            out_ref[rows, block] = total.astype(BF)


def last_mixed(q, w, m, y):
    return pl.pallas_call(
        last_mixed_kernel,
        in_specs=[VMEM] * 4,
        out_specs=VMEM,
        out_shape=shape(TOK, COLS, kind=BF),
        compiler_params=params(20),
        cost_estimate=cost(),
        name="last_mixed",
    )(q, w, m, y)


def local(*args):
    tie = lax.optimization_barrier
    args = args[:3] + (args[3].transpose(1, 0, 2),) + args[4:]
    q_hbm, v_hbm, e_hbm, gain, code = [pltpu.with_memory_space_constraint(a, pltpu.HBM) for a in args]
    w, q, qt, v, e, zf, own_f, oth_f = far_states(code, gain, q_hbm, v_hbm, e_hbm)
    got_f = send(oth_f, 1)
    zn, own_n, oth_n = near_states(qt, v, e, w)

    chip = [own_f[j] + got_f[j] for j in range(4)]
    chip, oth_n, v1 = tie((chip, oth_n, v))
    slices = [send(chip[j], 2 * j, 2 * (4 - j)) for j in (1, 2, 3)]
    got_n = send(oth_n, 1)
    near = [own_n[i] + got_n[i] for i in range(2)]
    ma, da, score, flipped, grad, z1, x1 = local_part(0, q, v1, e, w, (qt,))
    slices, near, grad = tie((slices, near, grad))
    mine = sum((s[0] for s in slices), chip[0][0])
    cross = sum((s[1:4] for s in slices), chip[0][1:4])
    pair = sum((s[4:6] for s in slices), chip[0][4:6])

    low = send(cross, 8)
    five = send(pair, 16)
    y2 = send(near[0], 2)
    y3 = [send(near[1], 6), send(near[1], 4)]
    low, five = tie((low, five))
    six = mine + low[0]
    six, v2 = tie((six, v1))
    y6 = [send(six, 32, 48), send(six, 48, 32)]
    mb, db, grad = local_part(1, q, v2, e, w, (score, flipped, grad))
    half = jnp.concatenate([(y6[0] + y6[1])[None], five])
    half, grad, v3 = tie((half, grad, v2))
    rest = send(half, 8)
    mc, dc, dq = local_part(2, q, v3, e, w, (score, flipped, grad))
    rest, dq = tie((rest, dq))
    quad = jnp.concatenate([half[0:1], rest[0:1], low[1:3], half[1:3] + rest[1:3]])
    quad, dq, x1, y2, y3 = tie((quad, dq, x1, y2, y3))
    y1 = send(x1, 1)
    y3 = y3[0] + y3[1]
    y23o = send(jnp.stack([y2, y3]), 1)
    pieces = [quad] + [send(quad, 2 * j, 2 * (4 - j)) for j in (1, 2, 3)]
    m, d, dq = mid_part(q, w, (ma, da, mb, db, mc, dc, dq), zn, z1, y1, y2, y3, y23o)
    for j in (1, 3, 2):
        pieces[j], dq = tie((pieces[j], dq))
    pieces = pieces + [send(p, 1) for p in pieces]
    top, low, y = score_part(dq, zf, pieces)
    got = [send_head(top, 1, 3), send_head(low, 3, 1)]
    grad_values = last_values(q, d, y)
    got, grad_values = tie((got, grad_values))
    top = top + got[0]
    low = low + got[1]
    top, low, m = tie((top, low, m))
    got = [send_head(top, 3, 1), send_head(low, 1, 3)]
    mixed = last_mixed(q, w, m, y)
    got, mixed = tie((got, mixed))
    grad_qk = jnp.concatenate([top + got[0], low + got[1]])
    return mixed, grad_qk, grad_values


def solution(mesh):
    placed = (P("seq", None), P("seq", "head"), P("seq", "head"), P(None, None, "head"), P("seq"))
    return jax.shard_map(
        local,
        mesh=mesh,
        in_specs=placed,
        out_specs=(P("seq", "head"), P("seq", None), P("seq", "head")),
        check_vma=False,
    )
```

```python
import functools

import jax
import jax.numpy as jnp
from jax import lax
from jax.experimental import pallas as pl
from jax.experimental.pallas import tpu as pltpu
from jax.sharding import PartitionSpec as P

HEAD_DIM = 64
CH = 64
TOK = 512
STATE = 128
COLS = 1280
HEADS = COLS // HEAD_DIM
BLK = 256
STEPS = COLS // BLK
SPANS = TOK // CH
USED = 10
TILE = 256
FIRST = 3
BF = jnp.bfloat16
F32 = jnp.float32
ROW, CORE, XMASK = 8, 1, 3
BLOCKS = tuple(slice(j * BLK, (j + 1) * BLK) for j in range(STEPS))

LOCAL = ((0, 0, 0), (0, 0, 1), (0, 0, 2), (1, 1, 0), (1, 1, 1), (1, 1, 2), (1, 0, 3))


def send(value, even, odd=None):
    odd = even if odd is None else odd
    pairs = [(source, source ^ (odd if source & CORE else even)) for source in range(lax.axis_size("seq"))]
    return lax.ppermute(value, "seq", pairs)


def send_head(value, even, odd):
    heads = lax.axis_size("head")
    pairs = []
    for source in range(lax.axis_size("seq")):
        for group in range(heads):
            target = group ^ (odd if source & CORE else even)
            pairs.append((source * heads + group, source * heads + target))
    return lax.ppermute(value, ("seq", "head"), pairs)


def neighbour(slot, core):
    return (slot * (1 + 2 * core)) & XMASK


def dot(a, b, over_a, over_b):
    return lax.dot_general(a, b, (((over_a,), (over_b,)), ((), ())), preferred_element_type=F32)


def coords():
    position = lax.axis_index("seq")
    return position, position & CORE, (position >> 1) & XMASK, (position >> 3) & CORE


def params(mib):
    return pltpu.CompilerParams(vmem_limit_bytes=mib * 1024 * 1024)


def cost():
    return pl.CostEstimate(flops=1024, bytes_accessed=1024, transcendentals=0)


def shape(*dims, kind=F32):
    return jax.ShapeDtypeStruct(dims, kind)


VMEM = pl.BlockSpec(memory_space=pltpu.VMEM)
SMEM = pl.BlockSpec(memory_space=pltpu.SMEM)
HBM = pl.BlockSpec(memory_space=pltpu.HBM)


def level_operand(z_ref, index, k, position, w_ref, v_ref, e_ref, block):
    upper = (position >> (k - 1)) & 1

    @pl.when(upper == 1)
    def _():
        for a in range(SPANS):
            rows = slice(a * CH, (a + 1) * CH)
            scaled = w_ref[k + 3, a : a + 1, block] * e_ref[rows, block].astype(F32)
            z_ref[index, rows, block] = scaled.astype(BF)

    @pl.when(upper == 0)
    def _():
        z_ref[index, :, block] = v_ref[:, block]


def far_kernel(
    code_hbm, gain_hbm, q_hbm, v_hbm, e_hbm, w_ref, q_ref, qt, v_ref, e_ref, z_ref, own_ref, oth_ref,
    code_ref, gain_ref, lw, res, sems
):
    position, core, x, z0 = coords()
    first = []
    for i, (far, near) in enumerate(((code_hbm, code_ref), (gain_hbm, gain_ref), (q_hbm, q_ref))):
        copy = pltpu.make_async_copy(far, near, sems.at[2 * STEPS + i])
        copy.start()
        first.append(copy)
    copies = []
    for j, block in enumerate(BLOCKS):
        for i, (far, near) in enumerate(((v_hbm, v_ref), (e_hbm, e_ref))):
            copy = pltpu.make_async_copy(far.at[:, block], near.at[:, block], sems.at[2 * j + i])
            copy.start()
            copies.append(copy)
    lw[...] = jnp.zeros_like(lw)
    for copy in first:
        copy.wait()
    for a in range(SPANS):
        lw[0:15, a : a + 1, 0:HEADS] = gain_ref[:, pl.ds(code_ref[a], 1), :]
    weights = lw[...].reshape(16 * SPANS, 128)[: USED * SPANS]
    high = weights.astype(BF)
    rest = weights - high.astype(F32)
    middle = rest.astype(BF)
    low = (rest - middle.astype(F32)).astype(BF)
    head = lax.broadcasted_iota(jnp.int32, (128, BLK), 0)
    for j, block in enumerate(BLOCKS):
        col = lax.broadcasted_iota(jnp.int32, (128, BLK), 1) + j * BLK
        spread = (head == col // HEAD_DIM).astype(BF)
        wide = dot(high, spread, 1, 0) + (dot(middle, spread, 1, 0) + dot(low, spread, 1, 0))
        w_ref[:, :, block] = wide.reshape(USED, SPANS, BLK)
    qt[...] = q_ref[...].T
    for j, block in enumerate(BLOCKS):
        copies[2 * j].wait()
        copies[2 * j + 1].wait()
        for index, k in enumerate((6, 4, 5)):
            level_operand(z_ref, index, k, position, w_ref, v_ref, e_ref, block)
            res[...] = dot(qt[...], z_ref[index, :, block], 1, 0).reshape(8, 2, ROW, BLK)
            for xr in range(4):
                for zr in range(2):
                    half = zr ^ z0 if k == 6 else zr
                    own_place = (core << 2) | (neighbour(xr, core) ^ x)
                    oth_place = ((core ^ 1) << 2) | (neighbour(xr, core ^ 1) ^ x)
                    own_ref[xr, 2 * index + zr, :, block] = res[own_place, half]
                    oth_ref[xr, 2 * index + zr, :, block] = res[oth_place, half]


def far_states(code, gain, q, v, e):
    return pl.pallas_call(
        far_kernel,
        in_specs=[HBM] * 5,
        out_specs=[VMEM] * 8,
        out_shape=[
            shape(USED, SPANS, COLS),
            shape(TOK, STATE, kind=BF),
            shape(STATE, TOK, kind=BF),
            shape(TOK, COLS, kind=BF),
            shape(TOK, COLS, kind=BF),
            shape(3, TOK, COLS, kind=BF),
            shape(4, 6, ROW, COLS),
            shape(4, 6, ROW, COLS),
        ],
        scratch_shapes=[
            pltpu.SMEM((SPANS,), jnp.int32),
            pltpu.VMEM((15, 16, HEADS), F32),
            pltpu.VMEM((16, SPANS, 128), F32),
            pltpu.VMEM((8, 2, ROW, BLK), F32),
            pltpu.SemaphoreType.DMA((2 * STEPS + 3,)),
        ],
        compiler_params=params(20),
        cost_estimate=cost(),
        name="far_states",
    )(code, gain, q, v, e)


def near_kernel(qt, v_ref, e_ref, w_ref, z_ref, own_ref, oth_ref, res):
    position, core, x, z0 = coords()
    for index, k in enumerate((2, 3)):
        for block in BLOCKS:
            level_operand(z_ref, index, k, position, w_ref, v_ref, e_ref, block)
            res[...] = dot(qt[...], z_ref[index, :, block], 1, 0).reshape(2, STATE // 2, BLK)
            own_ref[index, :, block] = res[core]
            oth_ref[index, :, block] = res[core ^ 1]


def near_states(qt, v, e, w):
    half = STATE // 2
    return pl.pallas_call(
        near_kernel,
        in_specs=[VMEM] * 4,
        out_specs=[VMEM] * 3,
        out_shape=[
            shape(2, TOK, COLS, kind=BF),
            shape(2, half, COLS),
            shape(2, half, COLS),
        ],
        scratch_shapes=[pltpu.VMEM((2, half, BLK), F32)],
        compiler_params=params(20),
        cost_estimate=cost(),
        name="near_states",
    )(qt, v, e, w)


def kept(level, flip):
    rows = lax.broadcasted_iota(jnp.int32, (TILE, TILE), 1 if flip else 0)
    keys = lax.broadcasted_iota(jnp.int32, (TILE, TILE), 0 if flip else 1)
    a, b = rows // CH, keys // CH
    if level == 0:
        return (a == b) & (keys <= rows)
    return ((a ^ b) >> (level - 1) == 1) & (a > b)


def add_outer(q_ref, w_ref, levels, position, y_ref, m_ref, d_ref, block):
    for index, k in enumerate(levels):

        @pl.when((position >> (k - 1)) & 1 == 1)
        def _():
            out = dot(q_ref[...], y_ref[index, :, block].astype(BF), 1, 0)
            for a in range(SPANS):
                rows = slice(a * CH, (a + 1) * CH)
                m_ref[rows, block] += w_ref[k + 3, a : a + 1, block] * out[rows, :]

    lower = None
    for index, k in enumerate(levels):
        part = (1 - ((position >> (k - 1)) & 1)).astype(F32) * y_ref[index, :, block]
        lower = part if lower is None else lower + part
    d_ref[:, block] += dot(q_ref[...], lower.astype(BF), 1, 0)


def local_blocks(first, count, v_ref, e_ref, w_ref, score, flipped, m_ref, d_ref, before, grad, z):
    per = TILE // CH

    def one_block(j, carry):
        block = pl.ds(pl.multiple_of((first + j) * BLK, BLK), BLK)
        out_block = pl.ds(pl.multiple_of(j * BLK, BLK), BLK)
        mixed = [None, None]
        d_val = [None, None]
        for index, (t, s, level) in enumerate(LOCAL):
            vals = v_ref[s * TILE : (s + 1) * TILE, block]
            for a in range(per):
                rows = slice(t * TILE + a * CH, t * TILE + (a + 1) * CH)
                w_row = w_ref[level, t * per + a : t * per + a + 1, block]
                z[index, a * CH : (a + 1) * CH, :] = (w_row * e_ref[rows, block].astype(F32)).astype(BF)
            out = dot(score[index], vals, 1, 0)
            w_rows = jnp.concatenate(
                [
                    jnp.broadcast_to(w_ref[level, t * per + a : t * per + a + 1, block], (CH, BLK))
                    for a in range(per)
                ],
                axis=0,
            )
            out = w_rows * out
            back = dot(flipped[index], z[index], 1, 0)
            mixed[t] = out if mixed[t] is None else mixed[t] + out
            d_val[s] = back if d_val[s] is None else d_val[s] + back
            grad[index] = before[index] + dot(z[index], vals, 1, 1)
        for i in range(2):
            m_ref[i * TILE : (i + 1) * TILE, out_block] = mixed[i]
            d_ref[i * TILE : (i + 1) * TILE, out_block] = d_val[i]
        return carry

    lax.fori_loop(0, count, one_block, 0)


def first_local_kernel(
    q_ref, v_ref, e_ref, w_ref, qt, m_ref, d_ref, score, flipped, grad, z1_ref, x1_ref, z
):
    position = lax.axis_index("seq")
    for block in BLOCKS:
        level_operand(z1_ref, 0, 1, position, w_ref, v_ref, e_ref, block)
        x1_ref[:, block] = dot(qt[...], z1_ref[0, :, block], 1, 0)
    grad[...] = jnp.zeros_like(grad)
    for index, (t, s, level) in enumerate(LOCAL):
        qt_rows = q_ref[t * TILE : (t + 1) * TILE, :]
        qs_rows = q_ref[s * TILE : (s + 1) * TILE, :]
        direct = dot(qt_rows, qs_rows, 1, 1)
        swapped = dot(qs_rows, qt_rows, 1, 1)
        if level < 3:
            direct = jnp.where(kept(level, False), direct, 0.0)
            swapped = jnp.where(kept(level, True), swapped, 0.0)
        score[index] = direct.astype(BF)
        flipped[index] = swapped.astype(BF)
    local_blocks(0, FIRST, v_ref, e_ref, w_ref, score, flipped, m_ref, d_ref, grad, grad, z)


def next_local_kernel(q_ref, v_ref, e_ref, w_ref, score, flipped, before, m_ref, d_ref, grad, z):
    local_blocks(FIRST, 1, v_ref, e_ref, w_ref, score, flipped, m_ref, d_ref, before, grad, z)


def end_local_kernel(q_ref, v_ref, e_ref, w_ref, score, flipped, before, m_ref, d_ref, dq_ref, grad, z):
    local_blocks(FIRST + 1, 1, v_ref, e_ref, w_ref, score, flipped, m_ref, d_ref, before, grad, z)
    q = [q_ref[i * TILE : (i + 1) * TILE, :] for i in range(2)]
    cross = grad[6].astype(BF)
    extra = [dot(cross, q[1], 0, 0), dot(cross, q[0], 1, 0)]
    for i in range(2):
        total = jnp.zeros((TILE, TILE), F32)
        for level in range(3):
            total = total + jnp.where(kept(level, False), grad[3 * i + level], 0.0)
        total = total.astype(BF)
        part = dot(total, q[i], 1, 0) + dot(total, q[i], 0, 0)
        dq_ref[i * TILE : (i + 1) * TILE, :] = part + extra[i]


def local_part(stage, q, v, e, w, tables):
    kernel = (first_local_kernel, next_local_kernel, end_local_kernel)[stage]
    wide = BLK if stage else FIRST * BLK
    table = shape(7, TILE, TILE, kind=BF)
    grad = shape(7, TILE, TILE)
    level_one = [shape(1, TOK, COLS, kind=BF), shape(STATE, COLS)]
    outs = ([table, table, grad] + level_one, [grad], [shape(TOK, STATE)])[stage]
    scratch = [pltpu.VMEM((7, TILE, BLK), BF)]
    if stage == 2:
        scratch = [pltpu.VMEM((7, TILE, TILE), F32)] + scratch
    return pl.pallas_call(
        kernel,
        in_specs=[VMEM] * (4 + len(tables)),
        out_specs=[VMEM] * (2 + len(outs)),
        out_shape=[shape(TOK, wide), shape(TOK, wide)] + outs,
        scratch_shapes=scratch,
        compiler_params=params(20),
        cost_estimate=pl.CostEstimate(flops=1 << 33, bytes_accessed=1 << 25, transcendentals=0),
        name=("first_local", "next_local", "end_local")[stage],
    )(q, v, e, w, *tables)


def mid_kernel(
    q_ref, w_ref, ma, da, mb, db, mc, dc, dq_in, z_ref, z1_ref, y1_ref, y2_ref, y3_ref, y23o_ref, m_ref, d_ref, dq_ref, y
):
    position, core, x, z0 = coords()
    half = STATE // 2
    own = pl.ds(pl.multiple_of(core * half, half), half)
    oth = pl.ds(pl.multiple_of((core ^ 1) * half, half), half)
    for index, ref in enumerate((y2_ref, y3_ref)):
        y[index, own, :] = ref[...]
        y[index, oth, :] = y23o_ref[index]
    y[2] = y1_ref[...]
    grads = dq_in[...]
    m_ref[:, : FIRST * BLK] = ma[...]
    d_ref[:, : FIRST * BLK] = da[...]
    m_ref[:, BLOCKS[FIRST]] = mb[...]
    d_ref[:, BLOCKS[FIRST]] = db[...]
    m_ref[:, BLOCKS[FIRST + 1]] = mc[...]
    d_ref[:, BLOCKS[FIRST + 1]] = dc[...]
    for block in BLOCKS:
        add_outer(q_ref, w_ref, (2, 3, 1), position, y, m_ref, d_ref, block)
        for index in range(3):
            z = z1_ref[0, :, block] if index == 2 else z_ref[index, :, block]
            grads = grads + dot(z, y[index, :, block].astype(BF), 1, 1)
    dq_ref[...] = grads


def mid_part(q, w, own, zn, z1, y1, y2, y3, y23o):
    return pl.pallas_call(
        mid_kernel,
        in_specs=[VMEM] * 15,
        out_specs=[VMEM] * 3,
        out_shape=[shape(TOK, COLS), shape(TOK, COLS), shape(TOK, STATE)],
        scratch_shapes=[pltpu.VMEM((3, STATE, COLS), F32)],
        compiler_params=params(30),
        cost_estimate=cost(),
        name="mid_part",
    )(q, w, *own, zn, z1, y1, y2, y3, y23o)


def score_kernel(*refs):
    dq_in, zf_ref = refs[:2]
    pieces = refs[2:10]
    top_ref, low_ref, y = refs[10:]
    position, core, x, z0 = coords()
    for cr in range(2):
        for xr in range(4):
            piece = pieces[4 * cr + xr]
            place = ((cr ^ core) << 2) | (neighbour(xr, cr ^ core) ^ x)
            rows = pl.ds(pl.multiple_of(place * 16, 16), 16)
            y[0, rows, :] = jnp.concatenate([piece[z0], piece[1 - z0]], axis=0)
            y[1, rows, :] = piece[2:4].reshape(16, COLS)
            y[2, rows, :] = piece[4:6].reshape(16, COLS)
    grads = dq_in[...]
    for block in BLOCKS:
        for index in range(3):
            grads = grads + dot(zf_ref[index, :, block], y[index, :, block].astype(BF), 1, 1)
    top_ref[...] = grads[: TOK // 2]
    low_ref[...] = grads[TOK // 2 :]


def score_part(dq, zf, pieces):
    part = shape(TOK // 2, STATE)
    return pl.pallas_call(
        score_kernel,
        in_specs=[VMEM] * 10,
        out_specs=[VMEM] * 3,
        out_shape=[part, part, shape(3, STATE, COLS)],
        compiler_params=params(20),
        cost_estimate=cost(),
        name="score_part",
    )(dq, zf, *pieces)


def last_values_kernel(q_ref, d_in, y_ref, out_ref):
    position = lax.axis_index("seq")
    for block in BLOCKS:
        lower = None
        for index, k in enumerate((6, 4, 5)):
            part = (1 - ((position >> (k - 1)) & 1)).astype(F32) * y_ref[index, :, block]
            lower = part if lower is None else lower + part
        out_ref[:, block] = (d_in[:, block] + dot(q_ref[...], lower.astype(BF), 1, 0)).astype(BF)


def last_values(q, d, y):
    return pl.pallas_call(
        last_values_kernel,
        in_specs=[VMEM] * 3,
        out_specs=VMEM,
        out_shape=shape(TOK, COLS, kind=BF),
        compiler_params=params(20),
        cost_estimate=cost(),
        name="last_values",
    )(q, d, y)


def last_mixed_kernel(q_ref, w_ref, m_in, y_ref, out_ref):
    position = lax.axis_index("seq")
    for block in BLOCKS:
        outs = [dot(q_ref[...], y_ref[index, :, block].astype(BF), 1, 0) for index in range(3)]
        for a in range(SPANS):
            rows = slice(a * CH, (a + 1) * CH)
            total = m_in[rows, block]
            for index, k in enumerate((6, 4, 5)):
                upper = ((position >> (k - 1)) & 1).astype(F32)
                total = total + (upper * w_ref[k + 3, a : a + 1, block]) * outs[index][rows, :]
            out_ref[rows, block] = total.astype(BF)


def last_mixed(q, w, m, y):
    return pl.pallas_call(
        last_mixed_kernel,
        in_specs=[VMEM] * 4,
        out_specs=VMEM,
        out_shape=shape(TOK, COLS, kind=BF),
        compiler_params=params(20),
        cost_estimate=cost(),
        name="last_mixed",
    )(q, w, m, y)


def local(*args):
    tie = lax.optimization_barrier
    args = args[:3] + (args[3].transpose(1, 0, 2),) + args[4:]
    q_hbm, v_hbm, e_hbm, gain, code = [pltpu.with_memory_space_constraint(a, pltpu.HBM) for a in args]
    w, q, qt, v, e, zf, own_f, oth_f = far_states(code, gain, q_hbm, v_hbm, e_hbm)
    got_f = send(oth_f, 1)
    zn, own_n, oth_n = near_states(qt, v, e, w)

    chip = [own_f[j] + got_f[j] for j in range(4)]
    chip, oth_n, v1 = tie((chip, oth_n, v))
    slices = [send(chip[j], 2 * j, 2 * (4 - j)) for j in (1, 2, 3)]
    got_n = send(oth_n, 1)
    near = [own_n[i] + got_n[i] for i in range(2)]
    ma, da, score, flipped, grad, z1, x1 = local_part(0, q, v1, e, w, (qt,))
    slices, near, grad = tie((slices, near, grad))
    mine = sum((s[0] for s in slices), chip[0][0])
    cross = sum((s[1:4] for s in slices), chip[0][1:4])
    pair = sum((s[4:6] for s in slices), chip[0][4:6])

    low = send(cross, 8)
    five = send(pair, 16)
    y2 = send(near[0], 2)
    y3 = [send(near[1], 6, 4), send(near[1], 4, 6)]
    low, five = tie((low, five))
    six = mine + low[0]
    six, v2 = tie((six, v1))
    y6 = [send(six, 32, 48), send(six, 48, 32)]
    mb, db, grad = local_part(1, q, v2, e, w, (score, flipped, grad))
    half = jnp.concatenate([(y6[0] + y6[1])[None], five])
    half, grad, v3 = tie((half, grad, v2))
    rest = send(half, 8)
    mc, dc, dq = local_part(2, q, v3, e, w, (score, flipped, grad))
    rest, dq = tie((rest, dq))
    quad = jnp.concatenate([half[0:1], rest[0:1], low[1:3], half[1:3] + rest[1:3]])
    quad, dq, x1, y2, y3 = tie((quad, dq, x1, y2, y3))
    y1 = send(x1, 1)
    y3 = y3[0] + y3[1]
    y23o = send(jnp.stack([y2, y3]), 1)
    pieces = [quad] + [send(quad, 2 * j, 2 * (4 - j)) for j in (1, 2, 3)]
    m, d, dq = mid_part(q, w, (ma, da, mb, db, mc, dc, dq), zn, z1, y1, y2, y3, y23o)
    for j in (1, 3, 2):
        pieces[j], dq = tie((pieces[j], dq))
    pieces = pieces + [send(p, 1) for p in pieces]
    top, low, y = score_part(dq, zf, pieces)
    got = [send_head(top, 1, 3), send_head(low, 3, 1)]
    grad_values = last_values(q, d, y)
    got, grad_values = tie((got, grad_values))
    top = top + got[0]
    low = low + got[1]
    top, low, m = tie((top, low, m))
    got = [send_head(top, 3, 1), send_head(low, 1, 3)]
    mixed = last_mixed(q, w, m, y)
    got, mixed = tie((got, mixed))
    grad_qk = jnp.concatenate([top + got[0], low + got[1]])
    return mixed, grad_qk, grad_values


def solution(mesh):
    placed = (P("seq", None), P("seq", "head"), P("seq", "head"), P(None, None, "head"), P("seq"))
    return jax.shard_map(
        local,
        mesh=mesh,
        in_specs=placed,
        out_specs=(P("seq", "head"), P("seq", None), P("seq", "head")),
        check_vma=False,
    )
```
